32 devices in a mesh: pix: 8 (over z, y), eb: 4 (over x, core).
Axes of the slice: x: 2, y: 2, z: 4, core: 2. Of those that a mesh axis runs over, the one named last changes fastest.
Arguments:
- abundance: float32 [8192, 1024], P('pix', 'eb'), may hold values from -60 to 60
- spectra: float32 [8192, 512], P('pix', 'eb'), may hold values from -6 to 6
- support: int32 [64, 16], P('pix', 'eb'), may hold values 0 or 1
- panel_blocks: int32 [2], replicated, may hold values from 0 to 15, as said below
Outputs:
- trailing: float32 [8192, 1024], P('pix', 'eb')
- residual: float32 [8192, 512], P('pix', 'eb')
- coefficients: float32 [2, 64, 512], P(None, None, 'eb')
The draws below stay inside these ranges and needn't reach their ends.
Inputs may be any that keep to these rules, and one draw needn't show every extreme that they name: `panel_blocks`: the 2 entries are different column blocks, and the last column block is always among them.
All inputs are finite; a program needn't handle non-finite values. No bound on the sum of `support` on one device may be relied on, other than what follows from the above.
Results may differ from the reference program's by a relative error of at most 0.00016.
Values sent between devices are 32-bit elements; how exact they have to be, the bound alone decides.
A program may use at most 64 MiB of HBM per device.

```python
import jax
import jax.numpy as jnp
from jax import lax

NCOL = 1024
BANDS = 512
PANEL = 64
TILE_ROWS = 128
NPANELS = 2
NROWS = 8192
NBLOCKS = 16


def draw_abundance(key, part):
    key_values = jax.random.fold_in(key, 11)
    key_rows = jax.random.fold_in(key, 12)
    key_cols = jax.random.fold_in(key, 13)
    values = jnp.clip(jax.random.normal(key_values, (NROWS, NCOL), jnp.float32), -5.0, 5.0)
    upper = 3.0
    tile_count = NROWS // TILE_ROWS
    tile_scale = jnp.exp(jax.random.uniform(key_rows, (tile_count, 1), jnp.float32, jnp.log(0.3), jnp.log(upper)))
    row_drift = 0.6 + 1.2 * jnp.arange(tile_count, dtype=jnp.float32)[:, None] / tile_count
    column_scale = jnp.exp(jax.random.uniform(key_cols, (1, NCOL), jnp.float32, jnp.log(0.5), jnp.log(2.0)))
    row_scale = jnp.repeat(tile_scale * row_drift, TILE_ROWS, axis=0)
    return values * row_scale * column_scale


def draw_panel_blocks(key, part):
    order = jax.random.permutation(jax.random.fold_in(key, 21), NBLOCKS - 1).astype(jnp.int32)
    chosen = order[:NPANELS]
    slot = jax.random.randint(jax.random.fold_in(key, 22), (), 0, NPANELS).astype(jnp.int32)
    places = jnp.arange(NPANELS, dtype=jnp.int32)
    return jnp.where(places == slot, jnp.int32(NBLOCKS - 1), chosen).astype(jnp.int32)


def plant(result, rng, low, top_value):
    place = [jax.random.randint(jax.random.fold_in(rng, axis), (), 0, length) for axis, length in enumerate(result.shape)]
    main_axis = result.shape.index(max(result.shape))
    beside = place[:main_axis] + [(place[main_axis] + 1) % result.shape[main_axis]] + place[main_axis + 1:]
    return result.at[tuple(place)].set(low).at[tuple(beside)].set(top_value)


def level_of(own_key, extent, shards, least, high):
    def one(position, shards_of):
        heights = jax.random.uniform(jax.random.fold_in(jax.random.fold_in(own_key, 6), position), (shards_of,), jnp.float32, least / len(shards), high / len(shards))
        return jnp.repeat(jnp.exp(heights), extent[position] // shards_of).reshape((-1,) + (1,) * (len(extent) - position - 1))

    level = one(*shards[0])
    for cut in shards[1:]:
        level = level * one(*cut)
    return level


def centred(own_key, shape, width, limit, cuts=(), kind=jnp.bfloat16):
    entries = jax.random.normal(own_key, shape, jnp.float32) * width
    if len(cuts) > 0:
        entries = level_of(own_key, shape, cuts, -0.22, 0.18) * entries
    return jnp.clip(entries, min=-limit, max=limit).astype(kind)


def setup_inputs(seed: int = 0) -> dict:
    arg_keys = jax.random.split(jax.random.key(seed), 5)
    abundance = draw_abundance(jax.random.fold_in(arg_keys[4], 71), 0)
    spectra = centred(arg_keys[1], (NROWS, BANDS), 1.0, 6.0, ((0, 8), (1, 4)), jnp.float32)
    support = plant((jax.random.randint(arg_keys[2], (NROWS // TILE_ROWS, NBLOCKS), 0, 4) < 3).astype(jnp.int32), jax.random.fold_in(arg_keys[2], 1), 0, 1)
    panel_blocks = draw_panel_blocks(jax.random.fold_in(arg_keys[4], 71), 0)
    return dict(abundance=abundance, spectra=spectra, support=support, panel_blocks=panel_blocks)


def product(left, right):
    return jnp.dot(left, right, precision=lax.Precision.HIGHEST)

def reference(abundance, spectra, support, panel_blocks):
    support_f = support.astype(jnp.float32)
    matrix_x = (abundance.reshape(NROWS // TILE_ROWS, TILE_ROWS, NBLOCKS, PANEL) * support_f[:, None, :, None]).reshape(NROWS, NCOL)
    matrix_y = spectra
    collected = []
    for panel_index in range(NPANELS):
        offset = (panel_blocks[panel_index] * PANEL).astype(jnp.int32)
        own_panel = lax.dynamic_slice_in_dim(matrix_x, offset, PANEL, 1)
        gram_sum = product(own_panel.T, own_panel)
        factor = jnp.linalg.cholesky(gram_sum)
        basis_t = jax.scipy.linalg.solve_triangular(factor, own_panel.T, lower=True)
        proj_a = product(basis_t, matrix_x)
        proj_b = product(basis_t, matrix_y)
        matrix_x = matrix_x - product(basis_t.T, proj_a)
        matrix_y = matrix_y - product(basis_t.T, proj_b)
        collected.append(proj_b)
    return (matrix_x, matrix_y, jnp.stack(collected))
```

```python
import functools

import jax
import jax.numpy as jnp
from jax import lax
from jax.experimental import pallas as pl
from jax.experimental.pallas import tpu as pltpu
from jax.sharding import PartitionSpec as P

PANEL = 64
TILE_ROWS = 128
NPANELS = 2
WIDTH = PANEL * NPANELS
SUB = 8
VMEM_LIMIT = 48 * 1024 * 1024


def product(left, right):
    return jnp.dot(left, right, precision=lax.Precision.HIGHEST, preferred_element_type=jnp.float32)


def product_t(left, right):
    return lax.dot_general(
        left,
        right,
        (((0,), (0,)), ((), ())),
        precision=lax.Precision.HIGHEST,
        preferred_element_type=jnp.float32,
    )


def support_row(support_ref, tile, cols):
    lane = lax.broadcasted_iota(jnp.int32, (1, cols), 1)
    row = jnp.zeros((1, cols), jnp.float32)
    for block in range(cols // PANEL):
        value = support_ref[tile, block].astype(jnp.float32)
        row = jnp.where((lane >= block * PANEL) & (lane < (block + 1) * PANEL), value, row)
    return row


def inverse_factor(work_ref):
    shape = (SUB, WIDTH)
    sublane = lax.broadcasted_iota(jnp.int32, shape, 0)
    for block in range(WIDTH // SUB):
        low = block * SUB
        rows_g = work_ref[low : low + SUB, :WIDTH]
        rows_t = work_ref[low : low + SUB, WIDTH:]
        columns = [jnp.broadcast_to(rows_g[:, low + j : low + j + 1], shape) for j in range(SUB)]
        entry = {
            (i, j): jnp.broadcast_to(columns[j][i : i + 1, :], shape)
            for j in range(SUB)
            for i in range(j, SUB)
        }
        g = [jnp.broadcast_to(rows_g[i : i + 1, :], shape) for i in range(SUB)]
        t = [jnp.broadcast_to(rows_t[i : i + 1, :], shape) for i in range(SUB)]
        upper = rows_g
        basis = rows_t
        for j in range(SUB):
            scale = lax.rsqrt(entry[j, j])
            for i in range(j + 1, SUB):
                entry[i, j] = entry[i, j] * scale
            g[j] = g[j] * scale
            t[j] = t[j] * scale
            for i in range(j + 1, SUB):
                for k in range(j + 1, i + 1):
                    entry[i, k] = entry[i, k] - entry[i, j] * entry[k, j]
                g[i] = g[i] - entry[i, j] * g[j]
                t[i] = t[i] - entry[i, j] * t[j]
            upper = jnp.where(sublane == j, g[j], upper)
            basis = jnp.where(sublane == j, t[j], basis)
        work_ref[low : low + SUB, WIDTH:] = basis
        if low + SUB < WIDTH:
            both = jnp.concatenate([upper, basis], axis=1)
            below = upper.T[low + SUB :, :]
            work_ref[low + SUB :, :] = work_ref[low + SUB :, :] - product(below, both)
    return work_ref[:, WIDTH:]


def gram_kernel(x_ref, y_ref, support_ref, c_ref, out_ref):
    rows, cols = x_ref.shape
    total = None
    for tile in range(rows // TILE_ROWS):
        span = pl.ds(tile * TILE_ROWS, TILE_ROWS)
        masked = x_ref[span, :] * support_row(support_ref, tile, cols)
        panel = c_ref[span, :]
        joined = jnp.concatenate([masked, y_ref[span, :], panel], axis=1)
        part = product_t(panel, joined)
        total = part if total is None else total + part
    out_ref[...] = total


def update_kernel(x_ref, y_ref, support_ref, c_ref, m_ref, trail_ref, resid_ref, coef_ref, work_ref):
    rows, cols = x_ref.shape
    bands = y_ref.shape[1]
    row = lax.broadcasted_iota(jnp.int32, (WIDTH, WIDTH), 0)
    col = lax.broadcasted_iota(jnp.int32, (WIDTH, WIDTH), 1)
    work_ref[:, :WIDTH] = m_ref[:, cols + bands :]
    work_ref[:, WIDTH:] = jnp.where(row == col, 1.0, 0.0).astype(jnp.float32)
    inverse = inverse_factor(work_ref)
    proj = product(inverse, m_ref[:, : cols + bands])
    coef_ref[...] = proj[:, cols:]
    weights = product_t(inverse, proj)
    for tile in range(rows // TILE_ROWS):
        span = pl.ds(tile * TILE_ROWS, TILE_ROWS)
        masked = x_ref[span, :] * support_row(support_ref, tile, cols)
        change = product(c_ref[span, :], weights)
        trail_ref[span, :] = masked - change[:, :cols]
        resid_ref[span, :] = y_ref[span, :] - change[:, cols:]


VMEM = pl.BlockSpec(memory_space=pltpu.VMEM)
SMEM = pl.BlockSpec(memory_space=pltpu.SMEM)


def own_panels(abundance, support, panel_blocks, holder):
    blocks_here = abundance.shape[1] // PANEL
    parts = []
    for index in range(NPANELS):
        block = panel_blocks[index]
        local = block % blocks_here
        panel = lax.dynamic_slice_in_dim(abundance, local * PANEL, PANEL, 1)
        keep = lax.dynamic_slice_in_dim(support, local, 1, 1).astype(jnp.float32)
        keep = jnp.where(block // blocks_here == holder, keep, 0.0)
        parts.append((panel.reshape(-1, TILE_ROWS, PANEL) * keep[:, :, None]).reshape(-1, PANEL))
    return jnp.concatenate(parts, axis=1)


def per_device(abundance, spectra, support, panel_blocks):
    rows, cols = abundance.shape
    bands = spectra.shape[1]
    own = own_panels(abundance, support, panel_blocks, lax.axis_index("eb"))
    panels = lax.psum(own, "eb")
    params = pltpu.CompilerParams(vmem_limit_bytes=VMEM_LIMIT)
    grams = pl.pallas_call(
        gram_kernel,
        out_shape=jax.ShapeDtypeStruct((WIDTH, cols + bands + WIDTH), jnp.float32),
        in_specs=[VMEM, VMEM, SMEM, VMEM],
        out_specs=VMEM,
        compiler_params=params,
        name="gram",
    )(abundance, spectra, support, panels)
    grams = lax.psum(grams, "pix")
    trailing, residual, coefficients = pl.pallas_call(
        update_kernel,
        out_shape=(
            jax.ShapeDtypeStruct((rows, cols), jnp.float32),
            jax.ShapeDtypeStruct((rows, bands), jnp.float32),
            jax.ShapeDtypeStruct((WIDTH, bands), jnp.float32),
        ),
        in_specs=[VMEM, VMEM, SMEM, VMEM, VMEM],
        out_specs=(VMEM, VMEM, VMEM),
        scratch_shapes=[pltpu.VMEM((WIDTH, 2 * WIDTH), jnp.float32)],
        compiler_params=params,
        name="update",
    )(abundance, spectra, support, panels, grams)
    return trailing, residual, coefficients.reshape(NPANELS, PANEL, bands)


def solution(mesh):
    placed = (P("pix", "eb"), P("pix", "eb"), P("pix", "eb"), P())
    return jax.shard_map(
        per_device,
        mesh=mesh,
        in_specs=placed,
        out_specs=(P("pix", "eb"), P("pix", "eb"), P(None, None, "eb")),
        check_vma=False,
    )
```

```python
import functools

import jax
import jax.numpy as jnp
from jax import lax
from jax.experimental import pallas as pl
from jax.experimental.pallas import tpu as pltpu
from jax.sharding import PartitionSpec as P

PANEL = 64
TILE_ROWS = 128
NPANELS = 2
WIDTH = PANEL * NPANELS
SUB = 8
VMEM_LIMIT = 48 * 1024 * 1024


def product(left, right):
    return jnp.dot(left, right, precision=lax.Precision.HIGHEST, preferred_element_type=jnp.float32)


def product_t(left, right):
    return lax.dot_general(
        left,
        right,
        (((0,), (0,)), ((), ())),
        precision=lax.Precision.HIGHEST,
        preferred_element_type=jnp.float32,
    )


def support_row(support_ref, tile, cols):
    lane = lax.broadcasted_iota(jnp.int32, (1, cols), 1)
    row = jnp.zeros((1, cols), jnp.float32)
    for block in range(cols // PANEL):
        value = support_ref[tile, block].astype(jnp.float32)
        row = jnp.where((lane >= block * PANEL) & (lane < (block + 1) * PANEL), value, row)
    return row


def inverse_factor(work_ref):
    shape = (SUB, WIDTH)
    sublane = lax.broadcasted_iota(jnp.int32, shape, 0)
    for block in range(WIDTH // SUB):
        low = block * SUB
        rows_g = work_ref[low : low + SUB, :WIDTH]
        rows_t = work_ref[low : low + SUB, WIDTH:]
        columns = [jnp.broadcast_to(rows_g[:, low + j : low + j + 1], shape) for j in range(SUB)]
        entry = {
            (i, j): jnp.broadcast_to(columns[j][i : i + 1, :], shape)
            for j in range(SUB)
            for i in range(j, SUB)
        }
        g = [jnp.broadcast_to(rows_g[i : i + 1, :], shape) for i in range(SUB)]
        t = [jnp.broadcast_to(rows_t[i : i + 1, :], shape) for i in range(SUB)]
        upper = rows_g
        basis = rows_t
        for j in range(SUB):
            scale = lax.rsqrt(entry[j, j])
            for i in range(j + 1, SUB):
                entry[i, j] = entry[i, j] * scale
            g[j] = g[j] * scale
            t[j] = t[j] * scale
            for i in range(j + 1, SUB):
                for k in range(j + 1, i + 1):
                    entry[i, k] = entry[i, k] - entry[i, j] * entry[k, j]
                g[i] = g[i] - entry[i, j] * g[j]
                t[i] = t[i] - entry[i, j] * t[j]
            upper = jnp.where(sublane == j, g[j], upper)
            basis = jnp.where(sublane == j, t[j], basis)
        work_ref[low : low + SUB, WIDTH:] = basis
        if low + SUB < WIDTH:
            both = jnp.concatenate([upper, basis], axis=1)
            below = upper.T[low + SUB :, :]
            work_ref[low + SUB :, :] = work_ref[low + SUB :, :] - product(below, both)
    return work_ref[:, WIDTH:]


def gram_kernel(x_ref, y_ref, support_ref, c_ref, out_ref):
    rows, cols = x_ref.shape
    total = None
    for tile in range(rows // TILE_ROWS):
        span = pl.ds(tile * TILE_ROWS, TILE_ROWS)
        masked = x_ref[span, :] * support_row(support_ref, tile, cols)
        panel = c_ref[span, :]
        joined = jnp.concatenate([masked, y_ref[span, :], panel], axis=1)
        part = product_t(panel, joined)
        total = part if total is None else total + part
    out_ref[...] = total


def update_kernel(x_ref, y_ref, support_ref, c_ref, m_ref, trail_ref, resid_ref, coef_ref, work_ref):
    rows, cols = x_ref.shape
    bands = y_ref.shape[1]
    row = lax.broadcasted_iota(jnp.int32, (WIDTH, WIDTH), 0)
    col = lax.broadcasted_iota(jnp.int32, (WIDTH, WIDTH), 1)
    work_ref[:, :WIDTH] = m_ref[:, cols + bands :]
    work_ref[:, WIDTH:] = jnp.where(row == col, 1.0, 0.0).astype(jnp.float32)
    inverse = inverse_factor(work_ref)
    proj = product(inverse, m_ref[:, : cols + bands])
    coef_ref[...] = proj[:, cols:]
    weights = product_t(inverse, proj)
    for tile in range(rows // TILE_ROWS):
        span = pl.ds(tile * TILE_ROWS, TILE_ROWS)
        masked = x_ref[span, :] * support_row(support_ref, tile, cols)
        change = product(c_ref[span, :], weights)
        trail_ref[span, :] = masked - change[:, :cols]
        resid_ref[span, :] = y_ref[span, :] - change[:, cols:]


def masked_tile(x_ref, support_ref, tile):
    span = pl.ds(pl.multiple_of(tile * TILE_ROWS, TILE_ROWS), TILE_ROWS)
    return x_ref[span, :] * support_row(support_ref, tile, x_ref.shape[1])


def own_panel_tile(x_ref, support_ref, blocks_ref, holder, tile):
    cols = x_ref.shape[1]
    blocks_here = cols // PANEL
    span = pl.ds(pl.multiple_of(tile * TILE_ROWS, TILE_ROWS), TILE_ROWS)
    left = lax.broadcasted_iota(jnp.int32, (1, WIDTH), 1) < PANEL
    total = jnp.zeros((TILE_ROWS, WIDTH), jnp.float32)
    for pair in range(cols // WIDTH):
        values = x_ref[span, pair * WIDTH : (pair + 1) * WIDTH]
        turned = pltpu.roll(values, PANEL, 1)
        factors = []
        for half in range(2):
            local = pair * 2 + half
            keep = support_ref[tile, local].astype(jnp.float32)
            factors.append(
                [jnp.where(blocks_ref[i] == holder * blocks_here + local, keep, 0.0) for i in range(2)]
            )
        straight = jnp.where(left, factors[0][0], factors[1][1])
        crossed = jnp.where(left, factors[1][0], factors[0][1])
        total = total + values * straight + turned * crossed
    return total


def exchange_kernel(
    pix_count,
    x_ref,
    y_ref,
    support_ref,
    blocks_ref,
    c_ref,
    m_ref,
    own,
    first_in,
    chip_sum,
    second_in,
    acc,
    slots,
    send1,
    recv1,
    send2,
    recv2,
    send3,
    recv3,
    send4,
    recv4,
    send5,
    recv5,
):
    rows, cols = x_ref.shape
    half = rows // 2
    chunks = half // TILE_ROWS
    pix = lax.axis_index("pix")
    eb = lax.axis_index("eb")
    core = eb % 2
    beside = eb + 1 - 2 * core
    across = (eb + 2) % 4
    others = [(pix + d) % pix_count for d in range(1, pix_count)]

    barrier = pltpu.get_barrier_semaphore()
    for target in [(pix, beside), (pix, across)] + [(other, eb) for other in others]:
        pl.semaphore_signal(barrier, inc=1, device_id=target, device_id_type=pl.DeviceIdType.MESH)

    def send(src, dst, send_sem, recv_sem, target):
        copy = pltpu.make_async_remote_copy(
            src_ref=src,
            dst_ref=dst,
            send_sem=send_sem,
            recv_sem=recv_sem,
            device_id=target,
            device_id_type=pl.DeviceIdType.MESH,
        )
        copy.start()
        return copy

    def span(side, chunk):
        start = pl.multiple_of((side * chunks + chunk) * TILE_ROWS, TILE_ROWS)
        return pl.ds(start, TILE_ROWS)

    def piece(chunk):
        return pl.ds(chunk * TILE_ROWS, TILE_ROWS)

    def prepare(side, chunk):
        tile = side * chunks + chunk
        own[span(side, chunk), :] = own_panel_tile(x_ref, support_ref, blocks_ref, eb, tile)

    def accumulate(side, chunk, first):
        panel = c_ref[span(side, chunk), :]
        masked = masked_tile(x_ref, support_ref, side * chunks + chunk)
        joined = jnp.concatenate([masked, y_ref[span(side, chunk), :], panel], axis=1)
        part = product_t(panel, joined)
        if first:
            acc[...] = part
        else:
            acc[...] += part

    other_core = 1 - core
    prepare(other_core, 0)
    pl.semaphore_wait(barrier, pix_count + 1)
    copies1 = []
    for chunk in range(chunks):
        if chunk > 0:
            prepare(other_core, chunk)
        copies1.append(
            send(
                own.at[span(other_core, chunk), :],
                first_in.at[piece(chunk), :],
                send1.at[chunk],
                recv1.at[chunk],
                (pix, beside),
            )
        )
    for chunk in range(chunks):
        prepare(core, chunk)

    copies2 = []
    for chunk in range(chunks):
        copies1[chunk].wait_recv()
        chip_sum[piece(chunk), :] = own[span(core, chunk), :] + first_in[piece(chunk), :]
        copies2.append(
            send(
                chip_sum.at[piece(chunk), :],
                second_in.at[piece(chunk), :],
                send2.at[chunk],
                recv2.at[chunk],
                (pix, across),
            )
        )

    copies3 = []
    for chunk in range(chunks):
        copies2[chunk].wait_recv()
        c_ref[span(core, chunk), :] = chip_sum[piece(chunk), :] + second_in[piece(chunk), :]
        copies3.append(
            send(
                c_ref.at[span(core, chunk), :],
                c_ref.at[span(core, chunk), :],
                send3.at[chunk],
                recv3.at[chunk],
                (pix, beside),
            )
        )
        accumulate(core, chunk, chunk == 0)
        if chunk > 0:
            copies3[chunk - 1].wait_recv()
            accumulate(other_core, chunk - 1, False)
    copies3[chunks - 1].wait_recv()
    accumulate(other_core, chunks - 1, False)

    share = WIDTH // pix_count

    def rows_of(index):
        return pl.ds(pl.multiple_of(index * share, share), share)

    copies4 = []
    for index, other in enumerate(others):
        copies4.append(
            send(acc.at[rows_of(other), :], slots.at[index], send4.at[index], recv4.at[index], (other, eb))
        )
    total = acc[rows_of(pix), :]
    for index in range(pix_count - 1):
        copies4[index].wait_recv()
        total = total + slots[index]
    m_ref[rows_of(pix), :] = total
    copies5 = []
    for index, other in enumerate(others):
        copies5.append(
            send(m_ref.at[rows_of(pix), :], m_ref.at[rows_of(pix), :], send5.at[index], recv5.at[index], (other, eb))
        )
    for copy in copies5:
        copy.wait_recv()
    for copy in copies1 + copies2 + copies3 + copies4 + copies5:
        copy.wait_send()


VMEM = pl.BlockSpec(memory_space=pltpu.VMEM)
SMEM = pl.BlockSpec(memory_space=pltpu.SMEM)


def own_panels(abundance, support, panel_blocks, holder):
    blocks_here = abundance.shape[1] // PANEL
    parts = []
    for index in range(NPANELS):
        block = panel_blocks[index]
        local = block % blocks_here
        panel = lax.dynamic_slice_in_dim(abundance, local * PANEL, PANEL, 1)
        keep = lax.dynamic_slice_in_dim(support, local, 1, 1).astype(jnp.float32)
        keep = jnp.where(block // blocks_here == holder, keep, 0.0)
        parts.append((panel.reshape(-1, TILE_ROWS, PANEL) * keep[:, :, None]).reshape(-1, PANEL))
    return jnp.concatenate(parts, axis=1)


def sums_by_collectives(abundance, spectra, support, panel_blocks):
    cols = abundance.shape[1]
    bands = spectra.shape[1]
    own = own_panels(abundance, support, panel_blocks, lax.axis_index("eb"))
    panels = lax.psum(own, "eb")
    grams = pl.pallas_call(
        gram_kernel,
        out_shape=jax.ShapeDtypeStruct((WIDTH, cols + bands + WIDTH), jnp.float32),
        in_specs=[VMEM, VMEM, SMEM, VMEM],
        out_specs=VMEM,
        compiler_params=pltpu.CompilerParams(vmem_limit_bytes=VMEM_LIMIT),
        name="gram",
    )(abundance, spectra, support, panels)
    return panels, lax.psum(grams, "pix")


def sums_by_copies(pix_count, abundance, spectra, support, panel_blocks):
    rows, cols = abundance.shape
    width = cols + spectra.shape[1] + WIDTH
    half = rows // 2
    chunks = half // TILE_ROWS
    dma = pltpu.SemaphoreType.DMA
    near = [dma((chunks,))] * 6
    far = [dma((pix_count - 1,))] * 4
    return pl.pallas_call(
        functools.partial(exchange_kernel, pix_count),
        out_shape=(
            jax.ShapeDtypeStruct((rows, WIDTH), jnp.float32),
            jax.ShapeDtypeStruct((WIDTH, width), jnp.float32),
        ),
        in_specs=[VMEM, VMEM, SMEM, SMEM],
        out_specs=(VMEM, VMEM),
        scratch_shapes=[
            pltpu.VMEM((rows, WIDTH), jnp.float32),
            pltpu.VMEM((half, WIDTH), jnp.float32),
            pltpu.VMEM((half, WIDTH), jnp.float32),
            pltpu.VMEM((half, WIDTH), jnp.float32),
            pltpu.VMEM((WIDTH, width), jnp.float32),
            pltpu.VMEM((pix_count - 1, WIDTH // pix_count, width), jnp.float32),
        ]
        + near
        + far,
        compiler_params=pltpu.CompilerParams(
            collective_id=0, has_side_effects=True, vmem_limit_bytes=VMEM_LIMIT
        ),
        name="exchange",
    )(abundance, spectra, support, panel_blocks)


def per_device(pix_count, eb_count, abundance, spectra, support, panel_blocks):
    rows, cols = abundance.shape
    bands = spectra.shape[1]
    args = (abundance, spectra, support, panel_blocks)
    if eb_count == 4 and 1 < pix_count and WIDTH % (SUB * pix_count) == 0:
        panels, grams = sums_by_copies(pix_count, *args)
    else:
        panels, grams = sums_by_collectives(*args)
    params = pltpu.CompilerParams(vmem_limit_bytes=VMEM_LIMIT)
    trailing, residual, coefficients = pl.pallas_call(
        update_kernel,
        out_shape=(
            jax.ShapeDtypeStruct((rows, cols), jnp.float32),
            jax.ShapeDtypeStruct((rows, bands), jnp.float32),
            jax.ShapeDtypeStruct((WIDTH, bands), jnp.float32),
        ),
        in_specs=[VMEM, VMEM, SMEM, VMEM, VMEM],
        out_specs=(VMEM, VMEM, VMEM),
        scratch_shapes=[pltpu.VMEM((WIDTH, 2 * WIDTH), jnp.float32)],
        compiler_params=params,
        name="update",
    )(abundance, spectra, support, panels, grams)
    return trailing, residual, coefficients.reshape(NPANELS, PANEL, bands)


def solution(mesh):
    placed = (P("pix", "eb"), P("pix", "eb"), P("pix", "eb"), P())
    return jax.shard_map(
        functools.partial(per_device, mesh.shape["pix"], mesh.shape["eb"]),
        mesh=mesh,
        in_specs=placed,
        out_specs=(P("pix", "eb"), P("pix", "eb"), P(None, None, "eb")),
        check_vma=False,
    )
```

```python
import functools

import jax
import jax.numpy as jnp
from jax import lax
from jax.experimental import pallas as pl
from jax.experimental.pallas import tpu as pltpu
from jax.sharding import PartitionSpec as P

PANEL = 64
TILE_ROWS = 128
NPANELS = 2
WIDTH = PANEL * NPANELS
SUB = 8
VMEM_LIMIT = 48 * 1024 * 1024


def product(left, right):
    return jnp.dot(left, right, precision=lax.Precision.HIGHEST, preferred_element_type=jnp.float32)


def product_t(left, right):
    return lax.dot_general(
        left,
        right,
        (((0,), (0,)), ((), ())),
        precision=lax.Precision.HIGHEST,
        preferred_element_type=jnp.float32,
    )


def support_row(support_ref, tile, cols):
    lane = lax.broadcasted_iota(jnp.int32, (1, cols), 1)
    row = jnp.zeros((1, cols), jnp.float32)
    for block in range(cols // PANEL):
        value = support_ref[block, tile].astype(jnp.float32)
        row = jnp.where((lane >= block * PANEL) & (lane < (block + 1) * PANEL), value, row)
    return row


def start_factor(work_ref, gram):
    row = lax.broadcasted_iota(jnp.int32, (WIDTH, WIDTH), 0)
    col = lax.broadcasted_iota(jnp.int32, (WIDTH, WIDTH), 1)
    work_ref[:, :WIDTH] = gram
    work_ref[:, WIDTH:] = jnp.where(row == col, 1.0, 0.0).astype(jnp.float32)


def factor_steps(work_ref, first, last):
    shape = (SUB, WIDTH)

    def step(block, carry):
        sublane = lax.broadcasted_iota(jnp.int32, shape, 0)
        row = lax.broadcasted_iota(jnp.int32, (WIDTH, SUB), 0)
        low = pl.multiple_of(block * SUB, SUB)
        rows_g = work_ref[pl.ds(low, SUB), :WIDTH]
        rows_t = work_ref[pl.ds(low, SUB), WIDTH:]
        turned = pltpu.roll(rows_g, (WIDTH - low) % WIDTH, 1)
        columns = [jnp.broadcast_to(turned[:, j : j + 1], shape) for j in range(SUB)]
        entry = {
            (i, j): jnp.broadcast_to(columns[j][i : i + 1, :], shape)
            for j in range(SUB)
            for i in range(j, SUB)
        }
        g = [jnp.broadcast_to(rows_g[i : i + 1, :], shape) for i in range(SUB)]
        t = [jnp.broadcast_to(rows_t[i : i + 1, :], shape) for i in range(SUB)]
        upper = rows_g
        basis = rows_t
        for j in range(SUB):
            scale = lax.rsqrt(entry[j, j])
            for i in range(j + 1, SUB):
                entry[i, j] = entry[i, j] * scale
            g[j] = g[j] * scale
            t[j] = t[j] * scale
            for i in range(j + 1, SUB):
                for k in range(j + 1, i + 1):
                    entry[i, k] = entry[i, k] - entry[i, j] * entry[k, j]
                g[i] = g[i] - entry[i, j] * g[j]
                t[i] = t[i] - entry[i, j] * t[j]
            upper = jnp.where(sublane == j, g[j], upper)
            basis = jnp.where(sublane == j, t[j], basis)
        work_ref[pl.ds(low, SUB), WIDTH:] = basis
        both = jnp.concatenate([upper, basis], axis=1)
        below = jnp.where(row >= low + SUB, upper.T, 0.0)
        work_ref[...] = work_ref[...] - product(below, both)
        return carry

    lax.fori_loop(first, last, step, 0)


def gram_kernel(x_ref, y_ref, support_ref, c_ref, out_ref):
    rows, cols = x_ref.shape
    total = None
    for tile in range(rows // TILE_ROWS):
        panel = c_ref[tile_span(tile), :]
        masked = masked_tile(x_ref, support_ref, tile)
        joined = jnp.concatenate([masked, y_ref[tile_span(tile), :], panel], axis=1)
        part = product_t(panel, joined)
        total = part if total is None else total + part
    out_ref[...] = total


def factor_kernel(gram_ref, inverse_ref, work_ref):
    start_factor(work_ref, gram_ref[...])
    factor_steps(work_ref, 0, WIDTH // SUB)
    inverse_ref[...] = work_ref[:, WIDTH:]


def update_kernel(
    x_hbm,
    y_hbm,
    support_ref,
    c_ref,
    m_ref,
    inverse_ref,
    trail_hbm,
    resid_hbm,
    coef_ref,
    x_ref,
    y_ref,
    trail,
    resid,
    in_sem,
    trail_sem,
    resid_sem,
):
    rows, cols = x_ref.shape
    loads = [
        pltpu.make_async_copy(x_hbm, x_ref, in_sem.at[0]),
        pltpu.make_async_copy(y_hbm, y_ref, in_sem.at[1]),
    ]
    for copy in loads:
        copy.start()
    inverse = inverse_ref[...]
    proj = product(inverse, m_ref[...])
    coef_ref[...] = proj[:, cols:]
    weights = product_t(inverse, proj)
    for copy in loads:
        copy.wait()
    stores = []
    for tile in range(rows // TILE_ROWS):
        span = pl.ds(tile * TILE_ROWS, TILE_ROWS)
        change = product(c_ref[span, :], weights)
        trail[span, :] = masked_tile(x_ref, support_ref, tile) - change[:, :cols]
        resid[span, :] = y_ref[span, :] - change[:, cols:]
        stores.append(pltpu.make_async_copy(trail.at[span, :], trail_hbm.at[span, :], trail_sem.at[tile]))
        stores.append(pltpu.make_async_copy(resid.at[span, :], resid_hbm.at[span, :], resid_sem.at[tile]))
        stores[-2].start()
        stores[-1].start()
    for copy in stores:
        copy.wait()


def tile_span(tile):
    start = tile * TILE_ROWS
    return pl.ds(start if isinstance(start, int) else pl.multiple_of(start, TILE_ROWS), TILE_ROWS)


def masked_tile(x_ref, support_ref, tile):
    span = tile_span(tile)
    return x_ref[span, :] * support_row(support_ref, tile, x_ref.shape[1])


def own_panel_tile(x_ref, support_ref, blocks_ref, holder, tile):
    cols = x_ref.shape[1]
    blocks_here = cols // PANEL
    span = tile_span(tile)
    left = lax.broadcasted_iota(jnp.int32, (1, WIDTH), 1) < PANEL
    total = jnp.zeros((TILE_ROWS, WIDTH), jnp.float32)
    for pair in range(cols // WIDTH):
        values = x_ref[span, pair * WIDTH : (pair + 1) * WIDTH]
        turned = pltpu.roll(values, PANEL, 1)
        factors = []
        for half in range(2):
            local = pair * 2 + half
            keep = support_ref[local, tile].astype(jnp.float32)
            factors.append(
                [jnp.where(blocks_ref[i] == holder * blocks_here + local, keep, 0.0) for i in range(2)]
            )
        straight = jnp.where(left, factors[0][0], factors[1][1])
        crossed = jnp.where(left, factors[1][0], factors[0][1])
        total = total + values * straight + turned * crossed
    return total


def exchange_kernel(
    pix_count,
    x_hbm,
    y_hbm,
    support_ref,
    blocks_ref,
    c_ref,
    m_ref,
    inverse_ref,
    x_ref,
    y_ref,
    own,
    first_in,
    chip_sum,
    second_in,
    gram_part,
    gram,
    gram_slots,
    acc,
    slots,
    work_ref,
    in_sem,
    send1,
    recv1,
    send2,
    recv2,
    send3,
    recv3,
    send4,
    recv4,
    send5,
    recv5,
    send6,
    recv6,
    send7,
    recv7,
):
    rows, cols = x_ref.shape
    half = rows // 2
    chunks = half // TILE_ROWS
    pix = lax.axis_index("pix")
    eb = lax.axis_index("eb")
    core = eb % 2
    beside = eb + 1 - 2 * core
    across = (eb + 2) % 4
    others = [(pix + d) % pix_count for d in range(1, pix_count)]

    def side_of(ref, side):
        return ref.at[pl.ds(pl.multiple_of(side * half, TILE_ROWS), half), :]

    loads = []
    for index, (src, dst) in enumerate(
        [
            (side_of(x_hbm, 1 - core), side_of(x_ref, 1 - core)),
            (side_of(x_hbm, core), side_of(x_ref, core)),
            (y_hbm, y_ref),
        ]
    ):
        loads.append(pltpu.make_async_copy(src, dst, in_sem.at[index]))
        loads[-1].start()

    barrier = pltpu.get_barrier_semaphore()
    for target in [(pix, beside), (pix, across)] + [(other, eb) for other in others]:
        pl.semaphore_signal(barrier, inc=1, device_id=target, device_id_type=pl.DeviceIdType.MESH)

    def send(src, dst, send_sem, recv_sem, target):
        copy = pltpu.make_async_remote_copy(
            src_ref=src,
            dst_ref=dst,
            send_sem=send_sem,
            recv_sem=recv_sem,
            device_id=target,
            device_id_type=pl.DeviceIdType.MESH,
        )
        copy.start()
        return copy

    def span(side, chunk):
        start = pl.multiple_of((side * chunks + chunk) * TILE_ROWS, TILE_ROWS)
        return pl.ds(start, TILE_ROWS)

    def piece(chunk):
        return pl.ds(chunk * TILE_ROWS, TILE_ROWS)

    def prepare(side, chunk):
        tile = side * chunks + chunk
        own[span(side, chunk), :] = own_panel_tile(x_ref, support_ref, blocks_ref, eb, tile)

    def accumulate_gram(side, chunk, first):
        panel = c_ref[span(side, chunk), :]
        part = product_t(panel, panel)
        gram_part[...] = part if first else gram_part[...] + part

    def accumulate(side, chunk, first):
        panel = c_ref[span(side, chunk), :]
        masked = masked_tile(x_ref, support_ref, side * chunks + chunk)
        part = product_t(panel, jnp.concatenate([masked, y_ref[span(side, chunk), :]], axis=1))
        acc[...] = part if first else acc[...] + part

    other_core = 1 - core
    loads[0].wait()
    prepare(other_core, 0)
    pl.semaphore_wait(barrier, pix_count + 1)
    copies1 = []
    for chunk in range(chunks):
        if chunk > 0:
            prepare(other_core, chunk)
        copies1.append(
            send(
                own.at[span(other_core, chunk), :],
                first_in.at[piece(chunk), :],
                send1.at[chunk],
                recv1.at[chunk],
                (pix, beside),
            )
        )
    loads[1].wait()
    for chunk in range(chunks):
        prepare(core, chunk)
    loads[2].wait()

    copies2 = []
    for chunk in range(chunks):
        copies1[chunk].wait_recv()
        chip_sum[piece(chunk), :] = own[span(core, chunk), :] + first_in[piece(chunk), :]
        copies2.append(
            send(
                chip_sum.at[piece(chunk), :],
                second_in.at[piece(chunk), :],
                send2.at[chunk],
                recv2.at[chunk],
                (pix, across),
            )
        )

    copies3 = []
    for chunk in range(chunks):
        copies2[chunk].wait_recv()
        c_ref[span(core, chunk), :] = chip_sum[piece(chunk), :] + second_in[piece(chunk), :]
        copies3.append(
            send(
                c_ref.at[span(core, chunk), :],
                c_ref.at[span(core, chunk), :],
                send3.at[chunk],
                recv3.at[chunk],
                (pix, beside),
            )
        )
        accumulate_gram(core, chunk, chunk == 0)
        if chunk < chunks - 1:
            accumulate(core, chunk, chunk == 0)
        if chunk > 0:
            copies3[chunk - 1].wait_recv()
            accumulate_gram(other_core, chunk - 1, False)
            if chunk < chunks - 1:
                accumulate(other_core, chunk - 1, False)
    copies3[chunks - 1].wait_recv()
    accumulate_gram(other_core, chunks - 1, False)

    share = WIDTH // pix_count
    mine = pl.ds(pl.multiple_of(pix * share, share), share)

    def scatter(part, landing, send_sem, recv_sem):
        copies = []
        for index, other in enumerate(others):
            rows_there = pl.ds(pl.multiple_of(other * share, share), share)
            copies.append(
                send(part.at[rows_there, :], landing.at[index], send_sem.at[index], recv_sem.at[index], (other, eb))
            )
        return copies

    def add_up(part, landing, copies):
        total = part[mine, :]
        for index in range(pix_count - 1):
            copies[index].wait_recv()
            total = total + landing[index]
        return total

    def gather(ref, send_sem, recv_sem):
        return [
            send(ref.at[mine, :], ref.at[mine, :], send_sem.at[index], recv_sem.at[index], (other, eb))
            for index, other in enumerate(others)
        ]

    copies4 = scatter(gram_part, gram_slots, send4, recv4)
    accumulate(core, chunks - 1, chunks == 1)
    if chunks > 1:
        accumulate(other_core, chunks - 2, False)
    accumulate(other_core, chunks - 1, False)
    gram[mine, :] = add_up(gram_part, gram_slots, copies4)
    copies5 = gather(gram, send5, recv5)
    copies6 = scatter(acc, slots, send6, recv6)
    for copy in copies5:
        copy.wait_recv()
    start_factor(work_ref, gram[...])
    steps = WIDTH // SUB
    factor_steps(work_ref, 0, steps // 2)
    m_ref[mine, :] = add_up(acc, slots, copies6)
    copies7 = gather(m_ref, send7, recv7)
    factor_steps(work_ref, steps // 2, steps)
    inverse_ref[...] = work_ref[:, WIDTH:]
    for copy in copies7:
        copy.wait_recv()
    for copy in copies1 + copies2 + copies3 + copies4 + copies5 + copies6 + copies7:
        copy.wait_send()


VMEM = pl.BlockSpec(memory_space=pltpu.VMEM)
SMEM = pl.BlockSpec(memory_space=pltpu.SMEM)
HBM = pl.BlockSpec(memory_space=pltpu.HBM)


def own_panels(abundance, support, panel_blocks, holder):
    blocks_here = abundance.shape[1] // PANEL
    parts = []
    for index in range(NPANELS):
        block = panel_blocks[index]
        local = block % blocks_here
        panel = lax.dynamic_slice_in_dim(abundance, local * PANEL, PANEL, 1)
        keep = lax.dynamic_slice_in_dim(support, local, 1, 1).astype(jnp.float32)
        keep = jnp.where(block // blocks_here == holder, keep, 0.0)
        parts.append((panel.reshape(-1, TILE_ROWS, PANEL) * keep[:, :, None]).reshape(-1, PANEL))
    return jnp.concatenate(parts, axis=1)


def sums_by_collectives(abundance, spectra, support, panel_blocks):
    cols = abundance.shape[1]
    bands = spectra.shape[1]
    own = own_panels(abundance, support.T, panel_blocks, lax.axis_index("eb"))
    panels = lax.psum(own, "eb")
    grams = pl.pallas_call(
        gram_kernel,
        out_shape=jax.ShapeDtypeStruct((WIDTH, cols + bands + WIDTH), jnp.float32),
        in_specs=[VMEM, VMEM, SMEM, VMEM],
        out_specs=VMEM,
        compiler_params=pltpu.CompilerParams(vmem_limit_bytes=VMEM_LIMIT),
        name="gram",
    )(abundance, spectra, support, panels)
    grams = lax.psum(grams, "pix")
    inverse = pl.pallas_call(
        factor_kernel,
        out_shape=jax.ShapeDtypeStruct((WIDTH, WIDTH), jnp.float32),
        in_specs=[VMEM],
        out_specs=VMEM,
        scratch_shapes=[pltpu.VMEM((WIDTH, 2 * WIDTH), jnp.float32)],
        compiler_params=pltpu.CompilerParams(vmem_limit_bytes=VMEM_LIMIT),
        name="factor",
    )(grams[:, cols + bands :])
    return panels, grams[:, : cols + bands], inverse


def sums_by_copies(pix_count, abundance, spectra, support, panel_blocks):
    rows, cols = abundance.shape
    width = cols + spectra.shape[1]
    half = rows // 2
    chunks = half // TILE_ROWS
    dma = pltpu.SemaphoreType.DMA
    near = [dma((chunks,))] * 6
    far = [dma((pix_count - 1,))] * 8
    return pl.pallas_call(
        functools.partial(exchange_kernel, pix_count),
        out_shape=(
            jax.ShapeDtypeStruct((rows, WIDTH), jnp.float32),
            jax.ShapeDtypeStruct((WIDTH, width), jnp.float32),
            jax.ShapeDtypeStruct((WIDTH, WIDTH), jnp.float32),
        ),
        in_specs=[HBM, HBM, SMEM, SMEM],
        out_specs=(VMEM, VMEM, VMEM),
        scratch_shapes=[
            pltpu.VMEM(abundance.shape, jnp.float32),
            pltpu.VMEM(spectra.shape, jnp.float32),
            pltpu.VMEM((rows, WIDTH), jnp.float32),
            pltpu.VMEM((half, WIDTH), jnp.float32),
            pltpu.VMEM((half, WIDTH), jnp.float32),
            pltpu.VMEM((half, WIDTH), jnp.float32),
            pltpu.VMEM((WIDTH, WIDTH), jnp.float32),
            pltpu.VMEM((WIDTH, WIDTH), jnp.float32),
            pltpu.VMEM((pix_count - 1, WIDTH // pix_count, WIDTH), jnp.float32),
            pltpu.VMEM((WIDTH, width), jnp.float32),
            pltpu.VMEM((pix_count - 1, WIDTH // pix_count, width), jnp.float32),
            pltpu.VMEM((WIDTH, 2 * WIDTH), jnp.float32),
            dma((3,)),
        ]
        + near
        + far,
        compiler_params=pltpu.CompilerParams(
            collective_id=0, has_side_effects=True, vmem_limit_bytes=VMEM_LIMIT
        ),
        name="exchange",
    )(abundance, spectra, support, panel_blocks)


def per_device(pix_count, eb_count, abundance, spectra, support, panel_blocks):
    rows, cols = abundance.shape
    bands = spectra.shape[1]
    support = support.T
    args = (abundance, spectra, support, panel_blocks)
    if eb_count == 4 and 1 < pix_count and WIDTH % (SUB * pix_count) == 0:
        panels, grams, inverse = sums_by_copies(pix_count, *args)
    else:
        panels, grams, inverse = sums_by_collectives(*args)
    params = pltpu.CompilerParams(vmem_limit_bytes=VMEM_LIMIT)
    trailing, residual, coefficients = pl.pallas_call(
        update_kernel,
        out_shape=(
            jax.ShapeDtypeStruct((rows, cols), jnp.float32),
            jax.ShapeDtypeStruct((rows, bands), jnp.float32),
            jax.ShapeDtypeStruct((WIDTH, bands), jnp.float32),
        ),
        in_specs=[HBM, HBM, SMEM, VMEM, VMEM, VMEM],
        out_specs=(HBM, HBM, VMEM),
        scratch_shapes=[
            pltpu.VMEM((rows, cols), jnp.float32),
            pltpu.VMEM((rows, bands), jnp.float32),
            pltpu.VMEM((rows, cols), jnp.float32),
            pltpu.VMEM((rows, bands), jnp.float32),
            pltpu.SemaphoreType.DMA((2,)),
            pltpu.SemaphoreType.DMA((rows // TILE_ROWS,)),
            pltpu.SemaphoreType.DMA((rows // TILE_ROWS,)),
        ],
        compiler_params=params,
        name="update",
    )(abundance, spectra, support, panels, grams, inverse)
    return trailing, residual, coefficients.reshape(NPANELS, PANEL, bands)


def solution(mesh):
    placed = (P("pix", "eb"), P("pix", "eb"), P("pix", "eb"), P())
    return jax.shard_map(
        functools.partial(per_device, mesh.shape["pix"], mesh.shape["eb"]),
        mesh=mesh,
        in_specs=placed,
        out_specs=(P("pix", "eb"), P("pix", "eb"), P(None, None, "eb")),
        check_vma=False,
    )
```

```python
import functools

import jax
import jax.numpy as jnp
from jax import lax
from jax.experimental import pallas as pl
from jax.experimental.pallas import tpu as pltpu
from jax.sharding import PartitionSpec as P

PANEL = 64
TILE_ROWS = 128
NPANELS = 2
WIDTH = PANEL * NPANELS
SUB = 8
VMEM_LIMIT = 48 * 1024 * 1024
EXCHANGE_VMEM = 64 * 1024 * 1024 - 512 * 1024


def product(left, right):
    return jnp.dot(left, right, precision=lax.Precision.HIGHEST, preferred_element_type=jnp.float32)


def product_t(left, right):
    return lax.dot_general(
        left,
        right,
        (((0,), (0,)), ((), ())),
        precision=lax.Precision.HIGHEST,
        preferred_element_type=jnp.float32,
    )


def product_nt(left, right):
    return lax.dot_general(
        left,
        right,
        (((1,), (1,)), ((), ())),
        precision=lax.Precision.HIGHEST,
        preferred_element_type=jnp.float32,
    )


def support_row(support_ref, tile, cols):
    lane = lax.broadcasted_iota(jnp.int32, (1, cols), 1)
    row = jnp.zeros((1, cols), jnp.float32)
    for block in range(cols // PANEL):
        value = support_ref[block, tile].astype(jnp.float32)
        row = jnp.where((lane >= block * PANEL) & (lane < (block + 1) * PANEL), value, row)
    return row


def factor_steps(work_ref, first, last):
    shape = (SUB, WIDTH)

    def step(block, carry):
        sublane = lax.broadcasted_iota(jnp.int32, shape, 0)
        row = lax.broadcasted_iota(jnp.int32, (PANEL, SUB), 0)
        low = pl.multiple_of(block * SUB, SUB)
        rows = work_ref[pl.ds(low, SUB), :]
        turned = pltpu.roll(rows, (WIDTH - low) % WIDTH, 1)
        columns = [jnp.broadcast_to(turned[:, j : j + 1], shape) for j in range(SUB)]
        entry = {
            (i, j): jnp.broadcast_to(columns[j][i : i + 1, :], shape)
            for j in range(SUB)
            for i in range(j, SUB)
        }
        g = [jnp.broadcast_to(rows[i : i + 1, :], shape) for i in range(SUB)]
        upper = rows
        for j in range(SUB):
            scale = lax.rsqrt(entry[j, j])
            for i in range(j + 1, SUB):
                entry[i, j] = entry[i, j] * scale
            g[j] = g[j] * scale
            for i in range(j + 1, SUB):
                for k in range(j + 1, i + 1):
                    entry[i, k] = entry[i, k] - entry[i, j] * entry[k, j]
                g[i] = g[i] - entry[i, j] * g[j]
            upper = jnp.where(sublane == j, g[j], upper)
        below = jnp.where(row >= low + SUB, upper.T[:PANEL, :], 0.0)
        work_ref[...] = work_ref[...] - product(below, upper)
        work_ref[pl.ds(low, SUB), :] = upper
        return carry

    lax.fori_loop(first, last, step, 0)


def inverse_factor(work_ref, gram):
    row = lax.broadcasted_iota(jnp.int32, (PANEL, PANEL), 0)
    col = lax.broadcasted_iota(jnp.int32, (PANEL, PANEL), 1)
    work_ref[...] = jnp.concatenate([gram, jnp.where(row == col, 1.0, 0.0)], axis=1)
    factor_steps(work_ref, 0, PANEL // SUB)
    return work_ref[:, PANEL:]


def second_factor(work_ref, inverse0, grams1, inverse_ref):
    coupling = product_nt(grams1[:, :PANEL], inverse0)
    remainder = grams1[:, PANEL:] - product_nt(coupling, coupling)
    carried = product(coupling, inverse0)
    inverse_ref[:PANEL, :] = jnp.concatenate([inverse0, jnp.zeros_like(inverse0)], axis=1)
    inverse1 = inverse_factor(work_ref, remainder)
    inverse_ref[PANEL:, :] = jnp.concatenate([-product(inverse1, carried), inverse1], axis=1)


def gram_kernel(x_ref, y_ref, support_ref, c_ref, out_ref):
    rows, cols = x_ref.shape
    total = None
    for tile in range(rows // TILE_ROWS):
        panel = c_ref[tile_span(tile), :]
        masked = masked_tile(x_ref, support_ref, tile)
        joined = jnp.concatenate([masked, y_ref[tile_span(tile), :], panel], axis=1)
        part = product_t(panel, joined)
        total = part if total is None else total + part
    out_ref[...] = total


def factor_kernel(gram_ref, inverse_ref, work_ref):
    inverse0 = inverse_factor(work_ref, gram_ref[:PANEL, :PANEL])
    second_factor(work_ref, inverse0, gram_ref[PANEL:, :], inverse_ref)


def update_kernel(
    x_hbm,
    y_hbm,
    support_ref,
    c_hbm,
    m_ref,
    inverse_ref,
    trail_hbm,
    resid_hbm,
    coef_ref,
    x_ref,
    y_ref,
    c_ref,
    trail,
    resid,
    in_sem,
    trail_sem,
    resid_sem,
):
    rows, cols = x_ref.shape
    loads = [
        pltpu.make_async_copy(x_hbm, x_ref, in_sem.at[0]),
        pltpu.make_async_copy(y_hbm, y_ref, in_sem.at[1]),
        pltpu.make_async_copy(c_hbm, c_ref, in_sem.at[2]),
    ]
    for copy in loads:
        copy.start()
    inverse = inverse_ref[...]
    share = m_ref.shape[1] // NPANELS
    sums = jnp.concatenate(
        [m_ref[p, i * share : (i + 1) * share, :] for i in range(NPANELS) for p in range(m_ref.shape[0])], axis=0
    )
    proj = product(inverse, sums)
    coef_ref[...] = proj[:, cols:]
    weights = product_t(inverse, proj)
    for copy in loads:
        copy.wait()
    stores = []
    for tile in range(rows // TILE_ROWS):
        span = pl.ds(tile * TILE_ROWS, TILE_ROWS)
        change = product(c_ref[span, :], weights)
        trail[span, :] = masked_tile(x_ref, support_ref, tile) - change[:, :cols]
        resid[span, :] = y_ref[span, :] - change[:, cols:]
        stores.append(pltpu.make_async_copy(trail.at[span, :], trail_hbm.at[span, :], trail_sem.at[tile]))
        stores.append(pltpu.make_async_copy(resid.at[span, :], resid_hbm.at[span, :], resid_sem.at[tile]))
        stores[-2].start()
        stores[-1].start()
    for copy in stores:
        copy.wait()


def tile_span(tile):
    start = tile * TILE_ROWS
    return pl.ds(start if isinstance(start, int) else pl.multiple_of(start, TILE_ROWS), TILE_ROWS)


def masked_tile(x_ref, support_ref, tile):
    span = tile_span(tile)
    return x_ref[span, :] * support_row(support_ref, tile, x_ref.shape[1])


def own_panel_pair(x_ref, support_ref, blocks_ref, holder, tile):
    blocks_here = x_ref.shape[1] // PANEL
    left = lax.broadcasted_iota(jnp.int32, (1, WIDTH), 1) < PANEL
    totals = [jnp.zeros((TILE_ROWS, WIDTH), jnp.float32) for _ in range(NPANELS)]
    for place in range(2):
        for pair in range(blocks_here // 2):
            values = x_ref[tile_span(tile + place), pair * WIDTH : (pair + 1) * WIDTH]
            turned = pltpu.roll(values, PANEL, 1)
            for half in range(2):
                local = pair * 2 + half
                keep = support_ref[local, tile + place].astype(jnp.float32)
                source = values if half == place else turned
                for index in range(NPANELS):
                    factor = jnp.where(blocks_ref[index] == holder * blocks_here + local, keep, 0.0)
                    lanes = jnp.where(left, factor, 0.0) if place == 0 else jnp.where(left, 0.0, factor)
                    totals[index] = totals[index] + source * lanes
    return totals


def exchange_kernel(
    pix_count,
    x_hbm,
    y_hbm,
    support_ref,
    blocks_ref,
    c_hbm,
    m_ref,
    inverse_ref,
    x_ref,
    y_ref,
    c_ref,
    own,
    first_in,
    chip_sum,
    second_in,
    full,
    gram0_part,
    gram0,
    gram0_slots,
    gram1_part,
    gram1,
    gram1_slots,
    m0_part,
    m0_slots,
    m1_part,
    m1_slots,
    work_ref,
    in_sem,
    out_sem,
    send1,
    recv1,
    send2,
    recv2,
    send3,
    recv3,
    gram0_sems,
    gram1_sems,
    m0_sems,
    m1_sems,
    gather_sems,
):
    rows, cols = x_ref.shape
    half = rows // 2
    chunks = half // (2 * TILE_ROWS)
    pix = lax.axis_index("pix")
    eb = lax.axis_index("eb")
    core = eb % 2
    other_core = 1 - core
    beside = eb + 1 - 2 * core
    across = (eb + 2) % 4
    others = [(pix + d) % pix_count for d in range(1, pix_count)]

    def side_of(ref, side):
        return ref.at[pl.ds(pl.multiple_of(side * half, TILE_ROWS), half), :]

    loads = []
    for index, (src, dst) in enumerate(
        [
            (side_of(x_hbm, other_core), side_of(x_ref, other_core)),
            (side_of(x_hbm, core), side_of(x_ref, core)),
            (y_hbm, y_ref),
        ]
    ):
        loads.append(pltpu.make_async_copy(src, dst, in_sem.at[index]))
        loads[-1].start()

    barrier = pltpu.get_barrier_semaphore()
    for target in [(pix, beside), (pix, across)] + [(other, eb) for other in others]:
        pl.semaphore_signal(barrier, inc=1, device_id=target, device_id_type=pl.DeviceIdType.MESH)

    started = []

    def send(src, dst, send_sem, recv_sem, target):
        copy = pltpu.make_async_remote_copy(
            src_ref=src,
            dst_ref=dst,
            send_sem=send_sem,
            recv_sem=recv_sem,
            device_id=target,
            device_id_type=pl.DeviceIdType.MESH,
        )
        copy.start()
        started.append(copy)
        return copy

    def prepare(side, chunk):
        pair = side * chunks + chunk
        for index, values in enumerate(own_panel_pair(x_ref, support_ref, blocks_ref, eb, pair * 2)):
            own[index, pair] = values

    def pair_span(pair):
        return pl.ds(pl.multiple_of(pair * (2 * TILE_ROWS), 2 * TILE_ROWS), 2 * TILE_ROWS)

    def unpack(index, pair):
        packed = full[index, pair]
        lanes = slice(index * PANEL, (index + 1) * PANEL)
        c_ref[tile_span(pair * 2), lanes] = packed[:, :PANEL]
        c_ref[tile_span(pair * 2 + 1), lanes] = packed[:, PANEL:]

    def add_gram(index, pair, part, first):
        panel = c_ref[pair_span(pair), index * PANEL : (index + 1) * PANEL]
        value = product_t(panel, c_ref[pair_span(pair), :])
        part[...] = value if first else part[...] + value

    def add_products(index, part):
        total = None
        for pair in range(2 * chunks):
            panel = c_ref[pair * 2 * TILE_ROWS : (pair + 1) * 2 * TILE_ROWS, index * PANEL : (index + 1) * PANEL]
            masked = jnp.concatenate(
                [masked_tile(x_ref, support_ref, pair * 2 + place) for place in range(2)], axis=0
            )
            values = y_ref[pair * 2 * TILE_ROWS : (pair + 1) * 2 * TILE_ROWS, :]
            value = product_t(panel, jnp.concatenate([masked, values], axis=1))
            total = value if total is None else total + value
        part[...] = total

    share = PANEL // pix_count
    mine = pl.ds(pl.multiple_of(pix * share, share), share)

    def scatter(part, landing, sems):
        copies = []
        for index, other in enumerate(others):
            rows_there = pl.ds(pl.multiple_of(other * share, share), share)
            copies.append(
                send(part.at[rows_there, :], landing.at[index], sems.at[0, index], sems.at[1, index], (other, eb))
            )
        return copies

    def add_up(part, landing, copies):
        total = part[mine, :]
        for index in range(pix_count - 1):
            copies[index].wait_recv()
            total = total + landing[index]
        return total

    def gather(block, sems, place):
        return [
            send(block, block, sems.at[place, index], sems.at[place + 1, index], (other, eb))
            for index, other in enumerate(others)
        ]

    def arrive(index):
        part = gram0_part if index == 0 else gram1_part
        copies3 = []
        for chunk in range(chunks):
            copies2[index][chunk].wait_recv()
            pair = core * chunks + chunk
            full[index, pair] = chip_sum[index, chunk] + second_in[index, chunk]
            copies3.append(
                send(
                    full.at[index, pair],
                    full.at[index, pair],
                    send3.at[index, chunk],
                    recv3.at[index, chunk],
                    (pix, beside),
                )
            )
            unpack(index, pair)
            add_gram(index, pair, part, chunk == 0)
        for chunk in range(chunks):
            copies3[chunk].wait_recv()
            pair = other_core * chunks + chunk
            unpack(index, pair)
            add_gram(index, pair, part, False)

    c_ref[...] = jnp.zeros_like(c_ref)
    loads[0].wait()
    for chunk in range(chunks):
        prepare(other_core, chunk)
    pl.semaphore_wait(barrier, pix_count + 1)
    copies1 = [
        [
            send(
                own.at[index, other_core * chunks + chunk],
                first_in.at[index, chunk],
                send1.at[index, chunk],
                recv1.at[index, chunk],
                (pix, beside),
            )
            for chunk in range(chunks)
        ]
        for index in range(NPANELS)
    ]
    loads[1].wait()
    for chunk in range(chunks):
        prepare(core, chunk)
    copies2 = []
    for index in range(NPANELS):
        copies2.append([])
        for chunk in range(chunks):
            copies1[index][chunk].wait_recv()
            chip_sum[index, chunk] = own[index, core * chunks + chunk] + first_in[index, chunk]
            copies2[index].append(
                send(
                    chip_sum.at[index, chunk],
                    second_in.at[index, chunk],
                    send2.at[index, chunk],
                    recv2.at[index, chunk],
                    (pix, across),
                )
            )
    loads[2].wait()

    arrive(0)
    gram0_copies = scatter(gram0_part, gram0_slots, gram0_sems)
    add_products(0, m0_part)
    gram0[mine, :] = add_up(gram0_part, gram0_slots, gram0_copies)
    gram0_gather = gather(gram0.at[mine, :], gram0_sems, 2)
    m0_copies = scatter(m0_part, m0_slots, m0_sems)

    arrive(1)
    gram1_copies = scatter(gram1_part, gram1_slots, gram1_sems)
    keep_c = pltpu.make_async_copy(c_ref, c_hbm, out_sem)
    keep_c.start()
    add_products(1, m1_part)
    gram1[mine, :] = add_up(gram1_part, gram1_slots, gram1_copies)
    gram1_gather = gather(gram1.at[mine, :], gram1_sems, 2)
    m1_copies = scatter(m1_part, m1_slots, m1_sems)

    for copy in gram0_gather:
        copy.wait_recv()
    inverse0 = inverse_factor(work_ref, gram0[:, :PANEL])
    m_ref[pix, :share, :] = add_up(m0_part, m0_slots, m0_copies)
    m_ref[pix, share:, :] = add_up(m1_part, m1_slots, m1_copies)
    m_gather = gather(m_ref.at[pix], gather_sems, 0)
    for copy in gram1_gather:
        copy.wait_recv()
    second_factor(work_ref, inverse0, gram1[...], inverse_ref)
    for copy in m_gather:
        copy.wait_recv()
    for copy in started:
        copy.wait_send()
    keep_c.wait()


VMEM = pl.BlockSpec(memory_space=pltpu.VMEM)
SMEM = pl.BlockSpec(memory_space=pltpu.SMEM)
HBM = pl.BlockSpec(memory_space=pltpu.HBM)


def own_panels(abundance, support, panel_blocks, holder):
    blocks_here = abundance.shape[1] // PANEL
    parts = []
    for index in range(NPANELS):
        block = panel_blocks[index]
        local = block % blocks_here
        panel = lax.dynamic_slice_in_dim(abundance, local * PANEL, PANEL, 1)
        keep = lax.dynamic_slice_in_dim(support, local, 1, 1).astype(jnp.float32)
        keep = jnp.where(block // blocks_here == holder, keep, 0.0)
        parts.append((panel.reshape(-1, TILE_ROWS, PANEL) * keep[:, :, None]).reshape(-1, PANEL))
    return jnp.concatenate(parts, axis=1)


def sums_by_collectives(abundance, spectra, support, panel_blocks):
    cols = abundance.shape[1]
    bands = spectra.shape[1]
    own = own_panels(abundance, support.T, panel_blocks, lax.axis_index("eb"))
    panels = lax.psum(own, "eb")
    grams = pl.pallas_call(
        gram_kernel,
        out_shape=jax.ShapeDtypeStruct((WIDTH, cols + bands + WIDTH), jnp.float32),
        in_specs=[VMEM, VMEM, SMEM, VMEM],
        out_specs=VMEM,
        compiler_params=pltpu.CompilerParams(vmem_limit_bytes=VMEM_LIMIT),
        name="gram",
    )(abundance, spectra, support, panels)
    grams = lax.psum(grams, "pix")
    inverse = pl.pallas_call(
        factor_kernel,
        out_shape=jax.ShapeDtypeStruct((WIDTH, WIDTH), jnp.float32),
        in_specs=[VMEM],
        out_specs=VMEM,
        scratch_shapes=[pltpu.VMEM((PANEL, WIDTH), jnp.float32)],
        compiler_params=pltpu.CompilerParams(vmem_limit_bytes=VMEM_LIMIT),
        name="factor",
    )(grams[:, cols + bands :])
    return panels, grams[:, : cols + bands].reshape(1, WIDTH, cols + bands), inverse


def sums_by_copies(pix_count, abundance, spectra, support, panel_blocks):
    rows, cols = abundance.shape
    width = cols + spectra.shape[1]
    chunks = rows // (4 * TILE_ROWS)
    share = PANEL // pix_count
    away = pix_count - 1
    dma = pltpu.SemaphoreType.DMA

    def buffer(*shape):
        return pltpu.VMEM(shape, jnp.float32)

    return pl.pallas_call(
        functools.partial(exchange_kernel, pix_count),
        out_shape=(
            jax.ShapeDtypeStruct((rows, WIDTH), jnp.float32),
            jax.ShapeDtypeStruct((pix_count, NPANELS * share, width), jnp.float32),
            jax.ShapeDtypeStruct((WIDTH, WIDTH), jnp.float32),
        ),
        in_specs=[HBM, HBM, SMEM, SMEM],
        out_specs=(HBM, VMEM, VMEM),
        scratch_shapes=[
            buffer(*abundance.shape),
            buffer(*spectra.shape),
            buffer(rows, WIDTH),
            buffer(NPANELS, 2 * chunks, TILE_ROWS, WIDTH),
            buffer(NPANELS, chunks, TILE_ROWS, WIDTH),
            buffer(NPANELS, chunks, TILE_ROWS, WIDTH),
            buffer(NPANELS, chunks, TILE_ROWS, WIDTH),
            buffer(NPANELS, 2 * chunks, TILE_ROWS, WIDTH),
            buffer(PANEL, WIDTH),
            buffer(PANEL, WIDTH),
            buffer(away, share, WIDTH),
            buffer(PANEL, WIDTH),
            buffer(PANEL, WIDTH),
            buffer(away, share, WIDTH),
            buffer(PANEL, width),
            buffer(away, share, width),
            buffer(PANEL, width),
            buffer(away, share, width),
            buffer(PANEL, WIDTH),
            dma((3,)),
            dma,
        ]
        + [dma((NPANELS, chunks))] * 6
        + [dma((4, away)), dma((4, away)), dma((2, away)), dma((2, away)), dma((2, away))],
        compiler_params=pltpu.CompilerParams(
            collective_id=0, has_side_effects=True, vmem_limit_bytes=EXCHANGE_VMEM
        ),
        name="exchange",
    )(abundance, spectra, support, panel_blocks)


def per_device(pix_count, eb_count, abundance, spectra, support, panel_blocks):
    rows, cols = abundance.shape
    bands = spectra.shape[1]
    support = support.T
    args = (abundance, spectra, support, panel_blocks)
    if eb_count == 4 and 1 < pix_count and PANEL % (SUB * pix_count) == 0 and rows % (4 * TILE_ROWS) == 0:
        panels, grams, inverse = sums_by_copies(pix_count, *args)
    else:
        panels, grams, inverse = sums_by_collectives(*args)
    params = pltpu.CompilerParams(vmem_limit_bytes=EXCHANGE_VMEM)
    trailing, residual, coefficients = pl.pallas_call(
        update_kernel,
        out_shape=(
            jax.ShapeDtypeStruct((rows, cols), jnp.float32),
            jax.ShapeDtypeStruct((rows, bands), jnp.float32),
            jax.ShapeDtypeStruct((WIDTH, bands), jnp.float32),
        ),
        in_specs=[HBM, HBM, SMEM, HBM, VMEM, VMEM],
        out_specs=(HBM, HBM, VMEM),
        scratch_shapes=[
            pltpu.VMEM((rows, cols), jnp.float32),
            pltpu.VMEM((rows, bands), jnp.float32),
            pltpu.VMEM((rows, WIDTH), jnp.float32),
            pltpu.VMEM((rows, cols), jnp.float32),
            pltpu.VMEM((rows, bands), jnp.float32),
            pltpu.SemaphoreType.DMA((3,)),
            pltpu.SemaphoreType.DMA((rows // TILE_ROWS,)),
            pltpu.SemaphoreType.DMA((rows // TILE_ROWS,)),
        ],
        compiler_params=params,
        name="update",
    )(abundance, spectra, support, panels, grams, inverse)
    return trailing, residual, coefficients.reshape(NPANELS, PANEL, bands)


def solution(mesh):
    placed = (P("pix", "eb"), P("pix", "eb"), P("pix", "eb"), P())
    return jax.shard_map(
        functools.partial(per_device, mesh.shape["pix"], mesh.shape["eb"]),
        mesh=mesh,
        in_specs=placed,
        out_specs=(P("pix", "eb"), P("pix", "eb"), P(None, None, "eb")),
        check_vma=False,
    )
```

```python
import functools

import jax
import jax.numpy as jnp
from jax import lax
from jax.experimental import pallas as pl
from jax.experimental.pallas import tpu as pltpu
from jax.sharding import PartitionSpec as P

PANEL = 64
TILE_ROWS = 128
NPANELS = 2
WIDTH = PANEL * NPANELS
SUB = 8
VMEM_LIMIT = 48 * 1024 * 1024
EXCHANGE_VMEM = 64 * 1024 * 1024 - 512 * 1024


def product(left, right):
    return jnp.dot(left, right, precision=lax.Precision.HIGHEST, preferred_element_type=jnp.float32)


def product_t(left, right):
    return lax.dot_general(
        left,
        right,
        (((0,), (0,)), ((), ())),
        precision=lax.Precision.HIGHEST,
        preferred_element_type=jnp.float32,
    )


def product_nt(left, right):
    return lax.dot_general(
        left,
        right,
        (((1,), (1,)), ((), ())),
        precision=lax.Precision.HIGHEST,
        preferred_element_type=jnp.float32,
    )


def support_row(support_ref, tile, cols):
    lane = lax.broadcasted_iota(jnp.int32, (1, cols), 1)
    row = jnp.zeros((1, cols), jnp.float32)
    for block in range(cols // PANEL):
        value = support_ref[block, tile].astype(jnp.float32)
        row = jnp.where((lane >= block * PANEL) & (lane < (block + 1) * PANEL), value, row)
    return row


def factor_steps(work_ref, first, last):
    shape = (SUB, WIDTH)

    def step(block, carry):
        sublane = lax.broadcasted_iota(jnp.int32, shape, 0)
        row = lax.broadcasted_iota(jnp.int32, (PANEL, SUB), 0)
        low = pl.multiple_of(block * SUB, SUB)
        rows = work_ref[pl.ds(low, SUB), :]
        turned = pltpu.roll(rows, (WIDTH - low) % WIDTH, 1)
        columns = [jnp.broadcast_to(turned[:, j : j + 1], shape) for j in range(SUB)]
        entry = {
            (i, j): jnp.broadcast_to(columns[j][i : i + 1, :], shape)
            for j in range(SUB)
            for i in range(j, SUB)
        }
        g = [jnp.broadcast_to(rows[i : i + 1, :], shape) for i in range(SUB)]
        upper = rows
        for j in range(SUB):
            scale = lax.rsqrt(entry[j, j])
            for i in range(j + 1, SUB):
                entry[i, j] = entry[i, j] * scale
            g[j] = g[j] * scale
            for i in range(j + 1, SUB):
                for k in range(j + 1, i + 1):
                    entry[i, k] = entry[i, k] - entry[i, j] * entry[k, j]
                g[i] = g[i] - entry[i, j] * g[j]
            upper = jnp.where(sublane == j, g[j], upper)
        below = jnp.where(row >= low + SUB, upper.T[:PANEL, :], 0.0)
        work_ref[...] = work_ref[...] - product(below, upper)
        work_ref[pl.ds(low, SUB), :] = upper
        return carry

    lax.fori_loop(first, last, step, 0)


def start_factor(work_ref, gram):
    row = lax.broadcasted_iota(jnp.int32, (PANEL, PANEL), 0)
    col = lax.broadcasted_iota(jnp.int32, (PANEL, PANEL), 1)
    work_ref[...] = jnp.concatenate([gram, jnp.where(row == col, 1.0, 0.0)], axis=1)


def inverse_factor(work_ref, gram):
    start_factor(work_ref, gram)
    factor_steps(work_ref, 0, PANEL // SUB)
    return work_ref[:, PANEL:]


def second_factor(work_ref, inverse0, grams1, inverse_ref):
    coupling = product_nt(grams1[:, :PANEL], inverse0)
    remainder = grams1[:, PANEL:] - product_nt(coupling, coupling)
    carried = product(coupling, inverse0)
    inverse_ref[:PANEL, :] = jnp.concatenate([inverse0, jnp.zeros_like(inverse0)], axis=1)
    inverse1 = inverse_factor(work_ref, remainder)
    inverse_ref[PANEL:, :] = jnp.concatenate([-product(inverse1, carried), inverse1], axis=1)


def gram_kernel(x_ref, y_ref, support_ref, c_ref, out_ref):
    rows, cols = x_ref.shape
    total = None
    for tile in range(rows // TILE_ROWS):
        panel = c_ref[tile_span(tile), :]
        masked = masked_tile(x_ref, support_ref, tile)
        joined = jnp.concatenate([masked, y_ref[tile_span(tile), :], panel], axis=1)
        part = product_t(panel, joined)
        total = part if total is None else total + part
    out_ref[...] = total


def factor_kernel(gram_ref, inverse_ref, work_ref):
    inverse0 = inverse_factor(work_ref, gram_ref[:PANEL, :PANEL])
    second_factor(work_ref, inverse0, gram_ref[PANEL:, :], inverse_ref)


def update_kernel(
    x_hbm,
    y_hbm,
    support_ref,
    c_hbm,
    m_ref,
    inverse_ref,
    trail_hbm,
    resid_hbm,
    coef_ref,
    x_ref,
    y_ref,
    c_ref,
    trail,
    resid,
    in_sem,
    trail_sem,
    resid_sem,
):
    rows, cols = x_ref.shape
    loads = [
        pltpu.make_async_copy(x_hbm, x_ref, in_sem.at[0]),
        pltpu.make_async_copy(y_hbm, y_ref, in_sem.at[1]),
        pltpu.make_async_copy(c_hbm, c_ref, in_sem.at[2]),
    ]
    for copy in loads:
        copy.start()
    inverse = inverse_ref[...]
    share = m_ref.shape[1] // NPANELS
    sums = jnp.concatenate(
        [m_ref[p, i * share : (i + 1) * share, :] for i in range(NPANELS) for p in range(m_ref.shape[0])], axis=0
    )
    proj = product(inverse, sums)
    coef_ref[...] = proj[:, cols:]
    weights = product_t(inverse, proj)
    for copy in loads:
        copy.wait()
    stores = []
    for tile in range(rows // TILE_ROWS):
        span = pl.ds(tile * TILE_ROWS, TILE_ROWS)
        change = product(c_ref[span, :], weights)
        trail[span, :] = masked_tile(x_ref, support_ref, tile) - change[:, :cols]
        resid[span, :] = y_ref[span, :] - change[:, cols:]
        stores.append(pltpu.make_async_copy(trail.at[span, :], trail_hbm.at[span, :], trail_sem.at[tile]))
        stores.append(pltpu.make_async_copy(resid.at[span, :], resid_hbm.at[span, :], resid_sem.at[tile]))
        stores[-2].start()
        stores[-1].start()
    for copy in stores:
        copy.wait()


def tile_span(tile):
    start = tile * TILE_ROWS
    return pl.ds(start if isinstance(start, int) else pl.multiple_of(start, TILE_ROWS), TILE_ROWS)


def masked_tile(x_ref, support_ref, tile):
    span = tile_span(tile)
    return x_ref[span, :] * support_row(support_ref, tile, x_ref.shape[1])


def own_panel_pair(x_ref, support_ref, blocks_ref, holder, tile):
    blocks_here = x_ref.shape[1] // PANEL
    left = lax.broadcasted_iota(jnp.int32, (1, WIDTH), 1) < PANEL
    totals = [jnp.zeros((TILE_ROWS, WIDTH), jnp.float32) for _ in range(NPANELS)]
    for place in range(2):
        for pair in range(blocks_here // 2):
            values = x_ref[tile_span(tile + place), pair * WIDTH : (pair + 1) * WIDTH]
            turned = pltpu.roll(values, PANEL, 1)
            for half in range(2):
                local = pair * 2 + half
                keep = support_ref[local, tile + place].astype(jnp.float32)
                source = values if half == place else turned
                for index in range(NPANELS):
                    factor = jnp.where(blocks_ref[index] == holder * blocks_here + local, keep, 0.0)
                    lanes = jnp.where(left, factor, 0.0) if place == 0 else jnp.where(left, 0.0, factor)
                    totals[index] = totals[index] + source * lanes
    return totals


def exchange_kernel(
    pix_count,
    x_hbm,
    y_hbm,
    support_ref,
    blocks_ref,
    c_hbm,
    m_ref,
    inverse_ref,
    x_ref,
    y_ref,
    c_ref,
    own,
    first_in,
    chip_sum,
    second_in,
    full,
    gram0_part,
    gram0,
    gram0_slots,
    gram1_part,
    gram1,
    gram1_slots,
    m0_part,
    m0_slots,
    m1_part,
    m1_slots,
    work_ref,
    in_sem,
    out_sem,
    send1,
    recv1,
    send2,
    recv2,
    send3,
    recv3,
    gram0_sems,
    gram1_sems,
    m0_sems,
    m1_sems,
    gather_sems,
    near0_sems,
    near1_sems,
):
    rows, cols = x_ref.shape
    half = rows // 2
    chunks = half // (2 * TILE_ROWS)
    pix = lax.axis_index("pix")
    eb = lax.axis_index("eb")
    core = eb % 2
    other_core = 1 - core
    beside = eb + 1 - 2 * core
    across = (eb + 2) % 4
    others = [(pix + d) % pix_count for d in range(1, pix_count)]

    def side_of(ref, side):
        return ref.at[pl.ds(pl.multiple_of(side * half, TILE_ROWS), half), :]

    loads = []
    for index, (src, dst) in enumerate(
        [
            (side_of(x_hbm, other_core), side_of(x_ref, other_core)),
            (side_of(x_hbm, core), side_of(x_ref, core)),
            (y_hbm, y_ref),
        ]
    ):
        loads.append(pltpu.make_async_copy(src, dst, in_sem.at[index]))
        loads[-1].start()

    barrier = pltpu.get_barrier_semaphore()
    near = [(pix, (eb + d) % 4) for d in range(1, 4)]
    for target in near + [(other, eb) for other in others]:
        pl.semaphore_signal(barrier, inc=1, device_id=target, device_id_type=pl.DeviceIdType.MESH)

    started = []

    def send(src, dst, send_sem, recv_sem, target):
        copy = pltpu.make_async_remote_copy(
            src_ref=src,
            dst_ref=dst,
            send_sem=send_sem,
            recv_sem=recv_sem,
            device_id=target,
            device_id_type=pl.DeviceIdType.MESH,
        )
        copy.start()
        started.append(copy)
        return copy

    def prepare(side, chunk):
        pair = side * chunks + chunk
        for index, values in enumerate(own_panel_pair(x_ref, support_ref, blocks_ref, eb, pair * 2)):
            own[index, pair] = values

    def pair_span(pair):
        return pl.ds(pl.multiple_of(pair * (2 * TILE_ROWS), 2 * TILE_ROWS), 2 * TILE_ROWS)

    def unpack(index, pair):
        packed = full[index, pair]
        lanes = slice(index * PANEL, (index + 1) * PANEL)
        c_ref[tile_span(pair * 2), lanes] = packed[:, :PANEL]
        c_ref[tile_span(pair * 2 + 1), lanes] = packed[:, PANEL:]

    def add_gram(index, pair, part, first):
        panel = c_ref[pair_span(pair), index * PANEL : (index + 1) * PANEL]
        value = product_t(panel, c_ref[pair_span(pair), :])
        part[...] = value if first else part[...] + value

    def add_products(index, pair, part, first):
        panel = c_ref[pair_span(pair), index * PANEL : (index + 1) * PANEL]
        masked = jnp.concatenate([masked_tile(x_ref, support_ref, pair * 2 + place) for place in range(2)], axis=0)
        value = product_t(panel, jnp.concatenate([masked, y_ref[pair_span(pair), :]], axis=1))
        part[...] = value if first else part[...] + value

    share = PANEL // pix_count
    mine = pl.ds(pl.multiple_of(pix * share, share), share)

    def scatter(part, landing, sems):
        copies = []
        for index, other in enumerate(others):
            rows_there = pl.ds(pl.multiple_of(other * share, share), share)
            copies.append(
                send(part.at[rows_there, :], landing.at[index], sems.at[0, index], sems.at[1, index], (other, eb))
            )
        return copies

    def add_up(part, landing, copies):
        total = part[mine, :]
        for index in range(pix_count - 1):
            copies[index].wait_recv()
            total = total + landing[index]
        return total

    def gather(block, sems, place):
        return [
            send(block, block, sems.at[place, index], sems.at[place + 1, index], (other, eb))
            for index, other in enumerate(others)
        ]

    quarter = PANEL // 4
    here = pl.ds(pl.multiple_of(eb * quarter, quarter), quarter)

    def spread_gram(part, landing, sems):
        return [
            send(part.at[here, :], landing.at[index], sems.at[0, index], sems.at[1, index], (other, eb))
            for index, other in enumerate(others)
        ]

    def share_gram(part, landing, gram, copies, sems):
        total = part[here, :]
        for index in range(pix_count - 1):
            copies[index].wait_recv()
            total = total + landing[index]
        gram[here, :] = total
        return [
            send(gram.at[here, :], gram.at[here, :], sems.at[0, index], sems.at[1, index], target)
            for index, target in enumerate(near)
        ]

    def arrive(index, part):
        copies3 = []
        for chunk in range(chunks):
            copies2[index][chunk].wait_recv()
            pair = core * chunks + chunk
            full[index, pair] = chip_sum[index, chunk] + second_in[index, chunk]
            copies3.append(
                send(
                    full.at[index, pair],
                    full.at[index, pair],
                    send3.at[index, chunk],
                    recv3.at[index, chunk],
                    (pix, beside),
                )
            )
            unpack(index, pair)
            add_gram(index, pair, part, chunk == 0)
        for chunk in range(chunks):
            copies3[chunk].wait_recv()
            pair = other_core * chunks + chunk
            unpack(index, pair)
            add_gram(index, pair, part, False)

    c_ref[...] = jnp.zeros_like(c_ref)
    loads[0].wait()
    for chunk in range(chunks):
        prepare(other_core, chunk)
    pl.semaphore_wait(barrier, pix_count + 2)
    copies1 = [
        [
            send(
                own.at[index, other_core * chunks + chunk],
                first_in.at[index, chunk],
                send1.at[index, chunk],
                recv1.at[index, chunk],
                (pix, beside),
            )
            for chunk in range(chunks)
        ]
        for index in range(NPANELS)
    ]
    loads[1].wait()
    for chunk in range(chunks):
        prepare(core, chunk)
    copies2 = []
    for index in range(NPANELS):
        copies2.append([])
        for chunk in range(chunks):
            copies1[index][chunk].wait_recv()
            chip_sum[index, chunk] = own[index, core * chunks + chunk] + first_in[index, chunk]
            copies2[index].append(
                send(
                    chip_sum.at[index, chunk],
                    second_in.at[index, chunk],
                    send2.at[index, chunk],
                    recv2.at[index, chunk],
                    (pix, across),
                )
            )
    loads[2].wait()

    low_rows = pl.ds(0, share)
    high_rows = pl.ds(share, share)
    steps = PANEL // SUB

    arrive(0, gram0_part)
    gram0_copies = spread_gram(gram0_part, gram0_slots, gram0_sems)
    for pair in range(2 * chunks):
        add_products(0, pair, m0_part, pair == 0)
    m0_copies = scatter(m0_part, m0_slots, m0_sems)
    gram0_near = share_gram(gram0_part, gram0_slots, gram0, gram0_copies, near0_sems)

    arrive(1, gram1_part)
    gram1_copies = spread_gram(gram1_part, gram1_slots, gram1_sems)
    for pair in range(2 * chunks):
        add_products(1, pair, m1_part, pair == 0)
    m1_copies = scatter(m1_part, m1_slots, m1_sems)
    keep_c = pltpu.make_async_copy(c_ref, c_hbm, out_sem)
    keep_c.start()
    m_ref[pix, low_rows, :] = add_up(m0_part, m0_slots, m0_copies)
    m0_gather = gather(m_ref.at[pix, low_rows, :], gather_sems, 0)

    for copy in gram0_near:
        copy.wait_recv()
    start_factor(work_ref, gram0[:, :PANEL])
    factor_steps(work_ref, 0, steps // 2)
    gram1_near = share_gram(gram1_part, gram1_slots, gram1, gram1_copies, near1_sems)
    factor_steps(work_ref, steps // 2, steps)
    inverse0 = work_ref[:, PANEL:]
    m_ref[pix, high_rows, :] = add_up(m1_part, m1_slots, m1_copies)
    m1_gather = gather(m_ref.at[pix, high_rows, :], gather_sems, 2)
    for copy in gram1_near:
        copy.wait_recv()
    second_factor(work_ref, inverse0, gram1[...], inverse_ref)
    for copy in m0_gather + m1_gather:
        copy.wait_recv()
    for copy in started:
        copy.wait_send()
    keep_c.wait()


VMEM = pl.BlockSpec(memory_space=pltpu.VMEM)
SMEM = pl.BlockSpec(memory_space=pltpu.SMEM)
HBM = pl.BlockSpec(memory_space=pltpu.HBM)


def own_panels(abundance, support, panel_blocks, holder):
    blocks_here = abundance.shape[1] // PANEL
    parts = []
    for index in range(NPANELS):
        block = panel_blocks[index]
        local = block % blocks_here
        panel = lax.dynamic_slice_in_dim(abundance, local * PANEL, PANEL, 1)
        keep = lax.dynamic_slice_in_dim(support, local, 1, 1).astype(jnp.float32)
        keep = jnp.where(block // blocks_here == holder, keep, 0.0)
        parts.append((panel.reshape(-1, TILE_ROWS, PANEL) * keep[:, :, None]).reshape(-1, PANEL))
    return jnp.concatenate(parts, axis=1)


def sums_by_collectives(abundance, spectra, support, panel_blocks):
    cols = abundance.shape[1]
    bands = spectra.shape[1]
    own = own_panels(abundance, support.T, panel_blocks, lax.axis_index("eb"))
    panels = lax.psum(own, "eb")
    grams = pl.pallas_call(
        gram_kernel,
        out_shape=jax.ShapeDtypeStruct((WIDTH, cols + bands + WIDTH), jnp.float32),
        in_specs=[VMEM, VMEM, SMEM, VMEM],
        out_specs=VMEM,
        compiler_params=pltpu.CompilerParams(vmem_limit_bytes=VMEM_LIMIT),
        name="gram",
    )(abundance, spectra, support, panels)
    grams = lax.psum(grams, "pix")
    inverse = pl.pallas_call(
        factor_kernel,
        out_shape=jax.ShapeDtypeStruct((WIDTH, WIDTH), jnp.float32),
        in_specs=[VMEM],
        out_specs=VMEM,
        scratch_shapes=[pltpu.VMEM((PANEL, WIDTH), jnp.float32)],
        compiler_params=pltpu.CompilerParams(vmem_limit_bytes=VMEM_LIMIT),
        name="factor",
    )(grams[:, cols + bands :])
    return panels, grams[:, : cols + bands].reshape(1, WIDTH, cols + bands), inverse


def sums_by_copies(pix_count, abundance, spectra, support, panel_blocks):
    rows, cols = abundance.shape
    width = cols + spectra.shape[1]
    chunks = rows // (4 * TILE_ROWS)
    share = PANEL // pix_count
    away = pix_count - 1
    dma = pltpu.SemaphoreType.DMA

    def buffer(*shape):
        return pltpu.VMEM(shape, jnp.float32)

    return pl.pallas_call(
        functools.partial(exchange_kernel, pix_count),
        out_shape=(
            jax.ShapeDtypeStruct((rows, WIDTH), jnp.float32),
            jax.ShapeDtypeStruct((pix_count, NPANELS * share, width), jnp.float32),
            jax.ShapeDtypeStruct((WIDTH, WIDTH), jnp.float32),
        ),
        in_specs=[HBM, HBM, SMEM, SMEM],
        out_specs=(HBM, VMEM, VMEM),
        scratch_shapes=[
            buffer(*abundance.shape),
            buffer(*spectra.shape),
            buffer(rows, WIDTH),
            buffer(NPANELS, 2 * chunks, TILE_ROWS, WIDTH),
            buffer(NPANELS, chunks, TILE_ROWS, WIDTH),
            buffer(NPANELS, chunks, TILE_ROWS, WIDTH),
            buffer(NPANELS, chunks, TILE_ROWS, WIDTH),
            buffer(NPANELS, 2 * chunks, TILE_ROWS, WIDTH),
            buffer(PANEL, WIDTH),
            buffer(PANEL, WIDTH),
            buffer(away, PANEL // 4, WIDTH),
            buffer(PANEL, WIDTH),
            buffer(PANEL, WIDTH),
            buffer(away, PANEL // 4, WIDTH),
            buffer(PANEL, width),
            buffer(away, share, width),
            buffer(PANEL, width),
            buffer(away, share, width),
            buffer(PANEL, WIDTH),
            dma((3,)),
            dma,
        ]
        + [dma((NPANELS, chunks))] * 6
        + [dma((2, away))] * 4
        + [dma((4, away)), dma((2, 3)), dma((2, 3))],
        compiler_params=pltpu.CompilerParams(
            collective_id=0, has_side_effects=True, vmem_limit_bytes=EXCHANGE_VMEM
        ),
        name="exchange",
    )(abundance, spectra, support, panel_blocks)


def per_device(pix_count, eb_count, abundance, spectra, support, panel_blocks):
    rows, cols = abundance.shape
    bands = spectra.shape[1]
    support = support.T
    args = (abundance, spectra, support, panel_blocks)
    if eb_count == 4 and 1 < pix_count and PANEL % (SUB * pix_count) == 0 and rows % (4 * TILE_ROWS) == 0:
        panels, grams, inverse = sums_by_copies(pix_count, *args)
    else:
        panels, grams, inverse = sums_by_collectives(*args)
    params = pltpu.CompilerParams(vmem_limit_bytes=EXCHANGE_VMEM)
    trailing, residual, coefficients = pl.pallas_call(
        update_kernel,
        out_shape=(
            jax.ShapeDtypeStruct((rows, cols), jnp.float32),
            jax.ShapeDtypeStruct((rows, bands), jnp.float32),
            jax.ShapeDtypeStruct((WIDTH, bands), jnp.float32),
        ),
        in_specs=[HBM, HBM, SMEM, HBM, VMEM, VMEM],
        out_specs=(HBM, HBM, VMEM),
        scratch_shapes=[
            pltpu.VMEM((rows, cols), jnp.float32),
            pltpu.VMEM((rows, bands), jnp.float32),
            pltpu.VMEM((rows, WIDTH), jnp.float32),
            pltpu.VMEM((rows, cols), jnp.float32),
            pltpu.VMEM((rows, bands), jnp.float32),
            pltpu.SemaphoreType.DMA((3,)),
            pltpu.SemaphoreType.DMA((rows // TILE_ROWS,)),
            pltpu.SemaphoreType.DMA((rows // TILE_ROWS,)),
        ],
        compiler_params=params,
        name="update",
    )(abundance, spectra, support, panels, grams, inverse)
    return trailing, residual, coefficients.reshape(NPANELS, PANEL, bands)


def solution(mesh):
    placed = (P("pix", "eb"), P("pix", "eb"), P("pix", "eb"), P())
    return jax.shard_map(
        functools.partial(per_device, mesh.shape["pix"], mesh.shape["eb"]),
        mesh=mesh,
        in_specs=placed,
        out_specs=(P("pix", "eb"), P("pix", "eb"), P(None, None, "eb")),
        check_vma=False,
    )
```

```python
import functools

import jax
import jax.numpy as jnp
from jax import lax
from jax.experimental import pallas as pl
from jax.experimental.pallas import tpu as pltpu
from jax.sharding import PartitionSpec as P

PANEL = 64
TILE_ROWS = 128
NPANELS = 2
WIDTH = PANEL * NPANELS
SUB = 8
VMEM_LIMIT = 48 * 1024 * 1024
EXCHANGE_VMEM = 64 * 1024 * 1024 - 512 * 1024


def product(left, right):
    return jnp.dot(left, right, precision=lax.Precision.HIGHEST, preferred_element_type=jnp.float32)


def product_t(left, right):
    return lax.dot_general(
        left,
        right,
        (((0,), (0,)), ((), ())),
        precision=lax.Precision.HIGHEST,
        preferred_element_type=jnp.float32,
    )


def split(values):
    high = values.astype(jnp.bfloat16)
    return high, (values - high.astype(jnp.float32)).astype(jnp.bfloat16)


def plain(left, right):
    return jnp.dot(left, right, preferred_element_type=jnp.float32)


def product_nt(left, right):
    return lax.dot_general(
        left,
        right,
        (((1,), (1,)), ((), ())),
        precision=lax.Precision.HIGHEST,
        preferred_element_type=jnp.float32,
    )


def support_row(support_ref, tile, cols):
    lane = lax.broadcasted_iota(jnp.int32, (1, cols), 1)
    row = jnp.zeros((1, cols), jnp.float32)
    for block in range(cols // PANEL):
        value = support_ref[block, tile].astype(jnp.float32)
        row = jnp.where((lane >= block * PANEL) & (lane < (block + 1) * PANEL), value, row)
    return row


def inverse_factor(gram):
    shape = (SUB, WIDTH)
    count = PANEL // SUB
    sublane = lax.broadcasted_iota(jnp.int32, shape, 0)
    lane = lax.broadcasted_iota(jnp.int32, shape, 1)
    pad = jnp.concatenate([gram, jnp.zeros_like(gram)], axis=1)
    tiles = [
        pad[i * SUB : (i + 1) * SUB, :] + jnp.where(lane == sublane + (PANEL + i * SUB), 1.0, 0.0)
        for i in range(count)
    ]
    for block in range(count):
        low = block * SUB

        def spread(tile):
            return [jnp.broadcast_to(tile[:, low + j : low + j + 1], shape) for j in range(SUB)]

        rows = tiles[block]
        columns = spread(rows)
        below = {r: spread(tiles[r]) for r in range(block + 1, count)}
        entry = {
            (i, j): jnp.broadcast_to(columns[j][i : i + 1, :], shape)
            for j in range(SUB)
            for i in range(j, SUB)
        }
        g = [jnp.broadcast_to(rows[i : i + 1, :], shape) for i in range(SUB)]
        upper = rows
        for j in range(SUB):
            scale = lax.rsqrt(entry[j, j])
            for i in range(j + 1, SUB):
                entry[i, j] = entry[i, j] * scale
            g[j] = g[j] * scale
            for i in range(j + 1, SUB):
                for k in range(j + 1, i + 1):
                    entry[i, k] = entry[i, k] - entry[i, j] * entry[k, j]
                g[i] = g[i] - entry[i, j] * g[j]
            upper = jnp.where(sublane == j, g[j], upper)
            for r, column in below.items():
                column[j] = column[j] * scale
                for k in range(j + 1, SUB):
                    column[k] = column[k] - column[j] * entry[k, j]
                tiles[r] = tiles[r] - column[j] * g[j]
        tiles[block] = upper
    return jnp.concatenate(tiles, axis=0)[:, PANEL:]


def second_factor(inverse0, grams1, inverse_ref):
    coupling = product_nt(grams1[:, :PANEL], inverse0)
    remainder = grams1[:, PANEL:] - product_nt(coupling, coupling)
    carried = product(coupling, inverse0)
    inverse_ref[:PANEL, :] = jnp.concatenate([inverse0, jnp.zeros_like(inverse0)], axis=1)
    inverse1 = inverse_factor(remainder)
    inverse_ref[PANEL:, :] = jnp.concatenate([-product(inverse1, carried), inverse1], axis=1)


def gram_kernel(x_ref, y_ref, support_ref, c_ref, out_ref):
    rows, cols = x_ref.shape
    total = None
    for tile in range(rows // TILE_ROWS):
        panel = c_ref[tile_span(tile), :]
        masked = masked_tile(x_ref, support_ref, tile)
        joined = jnp.concatenate([masked, y_ref[tile_span(tile), :], panel], axis=1)
        part = product_t(panel, joined)
        total = part if total is None else total + part
    out_ref[...] = total


def factor_kernel(gram_ref, inverse_ref):
    inverse0 = inverse_factor(gram_ref[:PANEL, :PANEL])
    second_factor(inverse0, gram_ref[PANEL:, :], inverse_ref)


def update_kernel(
    x_hbm,
    y_hbm,
    support_ref,
    c_hbm,
    m_ref,
    inverse_ref,
    trail_hbm,
    resid_hbm,
    coef_ref,
    x_ref,
    y_ref,
    c_ref,
    trail,
    resid,
    in_sem,
    trail_sem,
    resid_sem,
):
    rows, cols = x_ref.shape
    loads = [
        pltpu.make_async_copy(x_hbm, x_ref, in_sem.at[0]),
        pltpu.make_async_copy(y_hbm, y_ref, in_sem.at[1]),
        pltpu.make_async_copy(c_hbm, c_ref, in_sem.at[2]),
    ]
    for copy in loads:
        copy.start()
    inverse = inverse_ref[...]
    share = m_ref.shape[1] // NPANELS
    sums = jnp.concatenate(
        [m_ref[p, i * share : (i + 1) * share, :] for i in range(NPANELS) for p in range(m_ref.shape[0])], axis=0
    )
    proj = product(inverse, sums)
    coef_ref[...] = proj[:, cols:]
    high, low = split(product_t(inverse, proj))
    weights = jnp.concatenate([high, high, low], axis=0)
    for copy in loads:
        copy.wait()
    stores = []
    for tile in range(rows // TILE_ROWS):
        span = pl.ds(tile * TILE_ROWS, TILE_ROWS)
        high, low = split(c_ref[span, :])
        change = plain(jnp.concatenate([high, low, high], axis=1), weights)
        trail[span, :] = masked_tile(x_ref, support_ref, tile) - change[:, :cols]
        resid[span, :] = y_ref[span, :] - change[:, cols:]
        stores.append(pltpu.make_async_copy(trail.at[span, :], trail_hbm.at[span, :], trail_sem.at[tile]))
        stores.append(pltpu.make_async_copy(resid.at[span, :], resid_hbm.at[span, :], resid_sem.at[tile]))
        stores[-2].start()
        stores[-1].start()
    for copy in stores:
        copy.wait()


def tile_span(tile):
    start = tile * TILE_ROWS
    return pl.ds(start if isinstance(start, int) else pl.multiple_of(start, TILE_ROWS), TILE_ROWS)


def masked_tile(x_ref, support_ref, tile):
    span = tile_span(tile)
    return x_ref[span, :] * support_row(support_ref, tile, x_ref.shape[1])


def own_panel_pair(x_ref, support_ref, blocks_ref, holder, tile):
    blocks_here = x_ref.shape[1] // PANEL
    left = lax.broadcasted_iota(jnp.int32, (1, WIDTH), 1) < PANEL
    totals = [jnp.zeros((TILE_ROWS, WIDTH), jnp.float32) for _ in range(NPANELS)]
    for place in range(2):
        for pair in range(blocks_here // 2):
            values = x_ref[tile_span(tile + place), pair * WIDTH : (pair + 1) * WIDTH]
            turned = pltpu.roll(values, PANEL, 1)
            for half in range(2):
                local = pair * 2 + half
                keep = support_ref[local, tile + place].astype(jnp.float32)
                source = values if half == place else turned
                for index in range(NPANELS):
                    factor = jnp.where(blocks_ref[index] == holder * blocks_here + local, keep, 0.0)
                    lanes = jnp.where(left, factor, 0.0) if place == 0 else jnp.where(left, 0.0, factor)
                    totals[index] = totals[index] + source * lanes
    return totals


def exchange_kernel(
    pix_count,
    x_hbm,
    y_hbm,
    support_ref,
    blocks_ref,
    c_hbm,
    m_ref,
    inverse_ref,
    x_ref,
    y_ref,
    c_ref,
    own,
    first_in,
    chip_sum,
    second_in,
    full,
    gram0_part,
    gram0,
    gram0_slots,
    gram1_part,
    gram1,
    gram1_slots,
    m0_part,
    m0_slots,
    m1_part,
    m1_slots,
    xy_high,
    xy_low,
    in_sem,
    out_sem,
    send1,
    recv1,
    send2,
    recv2,
    send3,
    recv3,
    gram0_sems,
    gram1_sems,
    m0_sems,
    m1_sems,
    gather_sems,
    near0_sems,
    near1_sems,
):
    rows, cols = x_ref.shape
    half = rows // 2
    chunks = half // (2 * TILE_ROWS)
    pix = lax.axis_index("pix")
    eb = lax.axis_index("eb")
    core = eb % 2
    other_core = 1 - core
    beside = eb + 1 - 2 * core
    across = (eb + 2) % 4
    others = [(pix + d) % pix_count for d in range(1, pix_count)]

    def side_of(ref, side):
        return ref.at[pl.ds(pl.multiple_of(side * half, TILE_ROWS), half), :]

    loads = []
    for index, (src, dst) in enumerate(
        [
            (side_of(x_hbm, other_core), side_of(x_ref, other_core)),
            (side_of(x_hbm, core), side_of(x_ref, core)),
            (y_hbm, y_ref),
        ]
    ):
        loads.append(pltpu.make_async_copy(src, dst, in_sem.at[index]))
        loads[-1].start()

    barrier = pltpu.get_barrier_semaphore()
    near = [(pix, (eb + d) % 4) for d in range(1, 4)]
    for target in near + [(other, eb) for other in others]:
        pl.semaphore_signal(barrier, inc=1, device_id=target, device_id_type=pl.DeviceIdType.MESH)

    started = []

    def send(src, dst, send_sem, recv_sem, target):
        copy = pltpu.make_async_remote_copy(
            src_ref=src,
            dst_ref=dst,
            send_sem=send_sem,
            recv_sem=recv_sem,
            device_id=target,
            device_id_type=pl.DeviceIdType.MESH,
        )
        copy.start()
        started.append(copy)
        return copy

    def prepare(side, chunk):
        pair = side * chunks + chunk
        for index, values in enumerate(own_panel_pair(x_ref, support_ref, blocks_ref, eb, pair * 2)):
            own[index, pair] = values

    def pair_span(pair):
        return pl.ds(pl.multiple_of(pair * (2 * TILE_ROWS), 2 * TILE_ROWS), 2 * TILE_ROWS)

    def unpack(index, pair):
        packed = full[index, pair]
        lanes = slice(index * PANEL, (index + 1) * PANEL)
        c_ref[tile_span(pair * 2), lanes] = packed[:, :PANEL]
        c_ref[tile_span(pair * 2 + 1), lanes] = packed[:, PANEL:]

    def add_gram(index, pair, part, first):
        panel = c_ref[pair_span(pair), index * PANEL : (index + 1) * PANEL]
        value = product_t(panel, c_ref[pair_span(pair), :])
        part[...] = value if first else part[...] + value

    def add_products(index, pair, part, first):
        panel = c_ref[pair_span(pair), index * PANEL : (index + 1) * PANEL]
        high, low = split(panel.T)
        both = plain(jnp.concatenate([high, low], axis=0), xy_high[pair_span(pair), :])
        value = both[:PANEL] + both[PANEL:] + plain(high, xy_low[pair_span(pair), :])
        part[...] = value if first else part[...] + value

    share = PANEL // pix_count
    mine = pl.ds(pl.multiple_of(pix * share, share), share)

    def scatter(part, landing, sems):
        copies = []
        for index, other in enumerate(others):
            rows_there = pl.ds(pl.multiple_of(other * share, share), share)
            copies.append(
                send(part.at[rows_there, :], landing.at[index], sems.at[0, index], sems.at[1, index], (other, eb))
            )
        return copies

    def add_up(part, landing, copies):
        total = part[mine, :]
        for index in range(pix_count - 1):
            copies[index].wait_recv()
            total = total + landing[index]
        return total

    def gather(block, sems, place):
        return [
            send(block, block, sems.at[place, index], sems.at[place + 1, index], (other, eb))
            for index, other in enumerate(others)
        ]

    quarter = PANEL // 4
    here = pl.ds(pl.multiple_of(eb * quarter, quarter), quarter)

    def spread_gram(part, landing, sems):
        return [
            send(part.at[here, :], landing.at[index], sems.at[0, index], sems.at[1, index], (other, eb))
            for index, other in enumerate(others)
        ]

    def share_gram(part, landing, gram, copies, sems):
        total = part[here, :]
        for index in range(pix_count - 1):
            copies[index].wait_recv()
            total = total + landing[index]
        gram[here, :] = total
        return [
            send(gram.at[here, :], gram.at[here, :], sems.at[0, index], sems.at[1, index], target)
            for index, target in enumerate(near)
        ]

    def arrive(index, part):
        copies3 = []
        for chunk in range(chunks):
            copies2[index][chunk].wait_recv()
            pair = core * chunks + chunk
            full[index, pair] = chip_sum[index, chunk] + second_in[index, chunk]
            copies3.append(
                send(
                    full.at[index, pair],
                    full.at[index, pair],
                    send3.at[index, chunk],
                    recv3.at[index, chunk],
                    (pix, beside),
                )
            )
            unpack(index, pair)
            add_gram(index, pair, part, chunk == 0)
        for chunk in range(chunks):
            copies3[chunk].wait_recv()
            pair = other_core * chunks + chunk
            unpack(index, pair)
            add_gram(index, pair, part, False)

    c_ref[...] = jnp.zeros_like(c_ref)
    loads[0].wait()
    for chunk in range(chunks):
        prepare(other_core, chunk)
    pl.semaphore_wait(barrier, pix_count + 2)
    copies1 = [
        [
            send(
                own.at[index, other_core * chunks + chunk],
                first_in.at[index, chunk],
                send1.at[index, chunk],
                recv1.at[index, chunk],
                (pix, beside),
            )
            for chunk in range(chunks)
        ]
        for index in range(NPANELS)
    ]
    loads[1].wait()
    for chunk in range(chunks):
        prepare(core, chunk)
    copies2 = []
    for index in range(NPANELS):
        copies2.append([])
        for chunk in range(chunks):
            copies1[index][chunk].wait_recv()
            chip_sum[index, chunk] = own[index, core * chunks + chunk] + first_in[index, chunk]
            copies2[index].append(
                send(
                    chip_sum.at[index, chunk],
                    second_in.at[index, chunk],
                    send2.at[index, chunk],
                    recv2.at[index, chunk],
                    (pix, across),
                )
            )
    loads[2].wait()
    for tile in range(rows // TILE_ROWS):
        for values, lanes in [
            (masked_tile(x_ref, support_ref, tile), slice(0, cols)),
            (y_ref[tile_span(tile), :], slice(cols, None)),
        ]:
            high, low = split(values)
            xy_high[tile_span(tile), lanes] = high
            xy_low[tile_span(tile), lanes] = low

    low_rows = pl.ds(0, share)
    high_rows = pl.ds(share, share)

    arrive(0, gram0_part)
    gram0_copies = spread_gram(gram0_part, gram0_slots, gram0_sems)
    for pair in range(2 * chunks):
        add_products(0, pair, m0_part, pair == 0)
    m0_copies = scatter(m0_part, m0_slots, m0_sems)
    gram0_near = share_gram(gram0_part, gram0_slots, gram0, gram0_copies, near0_sems)

    arrive(1, gram1_part)
    gram1_copies = spread_gram(gram1_part, gram1_slots, gram1_sems)
    for pair in range(2 * chunks):
        add_products(1, pair, m1_part, pair == 0)
    m1_copies = scatter(m1_part, m1_slots, m1_sems)
    keep_c = pltpu.make_async_copy(c_ref, c_hbm, out_sem)
    keep_c.start()
    m_ref[pix, low_rows, :] = add_up(m0_part, m0_slots, m0_copies)
    m0_gather = gather(m_ref.at[pix, low_rows, :], gather_sems, 0)

    for copy in gram0_near:
        copy.wait_recv()
    inverse0 = inverse_factor(gram0[:, :PANEL])
    gram1_near = share_gram(gram1_part, gram1_slots, gram1, gram1_copies, near1_sems)
    m_ref[pix, high_rows, :] = add_up(m1_part, m1_slots, m1_copies)
    m1_gather = gather(m_ref.at[pix, high_rows, :], gather_sems, 2)
    for copy in gram1_near:
        copy.wait_recv()
    second_factor(inverse0, gram1[...], inverse_ref)
    for copy in m0_gather + m1_gather:
        copy.wait_recv()
    for copy in started:
        copy.wait_send()
    keep_c.wait()


VMEM = pl.BlockSpec(memory_space=pltpu.VMEM)
SMEM = pl.BlockSpec(memory_space=pltpu.SMEM)
HBM = pl.BlockSpec(memory_space=pltpu.HBM)


def own_panels(abundance, support, panel_blocks, holder):
    blocks_here = abundance.shape[1] // PANEL
    parts = []
    for index in range(NPANELS):
        block = panel_blocks[index]
        local = block % blocks_here
        panel = lax.dynamic_slice_in_dim(abundance, local * PANEL, PANEL, 1)
        keep = lax.dynamic_slice_in_dim(support, local, 1, 1).astype(jnp.float32)
        keep = jnp.where(block // blocks_here == holder, keep, 0.0)
        parts.append((panel.reshape(-1, TILE_ROWS, PANEL) * keep[:, :, None]).reshape(-1, PANEL))
    return jnp.concatenate(parts, axis=1)


def sums_by_collectives(abundance, spectra, support, panel_blocks):
    cols = abundance.shape[1]
    bands = spectra.shape[1]
    own = own_panels(abundance, support.T, panel_blocks, lax.axis_index("eb"))
    panels = lax.psum(own, "eb")
    grams = pl.pallas_call(
        gram_kernel,
        out_shape=jax.ShapeDtypeStruct((WIDTH, cols + bands + WIDTH), jnp.float32),
        in_specs=[VMEM, VMEM, SMEM, VMEM],
        out_specs=VMEM,
        compiler_params=pltpu.CompilerParams(vmem_limit_bytes=VMEM_LIMIT),
        name="gram",
    )(abundance, spectra, support, panels)
    grams = lax.psum(grams, "pix")
    inverse = pl.pallas_call(
        factor_kernel,
        out_shape=jax.ShapeDtypeStruct((WIDTH, WIDTH), jnp.float32),
        in_specs=[VMEM],
        out_specs=VMEM,
        compiler_params=pltpu.CompilerParams(vmem_limit_bytes=VMEM_LIMIT),
        name="factor",
    )(grams[:, cols + bands :])
    return panels, grams[:, : cols + bands].reshape(1, WIDTH, cols + bands), inverse


def sums_by_copies(pix_count, abundance, spectra, support, panel_blocks):
    rows, cols = abundance.shape
    width = cols + spectra.shape[1]
    chunks = rows // (4 * TILE_ROWS)
    share = PANEL // pix_count
    away = pix_count - 1
    dma = pltpu.SemaphoreType.DMA

    def buffer(*shape):
        return pltpu.VMEM(shape, jnp.float32)

    return pl.pallas_call(
        functools.partial(exchange_kernel, pix_count),
        out_shape=(
            jax.ShapeDtypeStruct((rows, WIDTH), jnp.float32),
            jax.ShapeDtypeStruct((pix_count, NPANELS * share, width), jnp.float32),
            jax.ShapeDtypeStruct((WIDTH, WIDTH), jnp.float32),
        ),
        in_specs=[HBM, HBM, SMEM, SMEM],
        out_specs=(HBM, VMEM, VMEM),
        scratch_shapes=[
            buffer(*abundance.shape),
            buffer(*spectra.shape),
            buffer(rows, WIDTH),
            buffer(NPANELS, 2 * chunks, TILE_ROWS, WIDTH),
            buffer(NPANELS, chunks, TILE_ROWS, WIDTH),
            buffer(NPANELS, chunks, TILE_ROWS, WIDTH),
            buffer(NPANELS, chunks, TILE_ROWS, WIDTH),
            buffer(NPANELS, 2 * chunks, TILE_ROWS, WIDTH),
            buffer(PANEL, WIDTH),
            buffer(PANEL, WIDTH),
            buffer(away, PANEL // 4, WIDTH),
            buffer(PANEL, WIDTH),
            buffer(PANEL, WIDTH),
            buffer(away, PANEL // 4, WIDTH),
            buffer(PANEL, width),
            buffer(away, share, width),
            buffer(PANEL, width),
            buffer(away, share, width),
            pltpu.VMEM((rows, width), jnp.bfloat16),
            pltpu.VMEM((rows, width), jnp.bfloat16),
            dma((3,)),
            dma,
        ]
        + [dma((NPANELS, chunks))] * 6
        + [dma((2, away))] * 4
        + [dma((4, away)), dma((2, 3)), dma((2, 3))],
        compiler_params=pltpu.CompilerParams(
            collective_id=0, has_side_effects=True, vmem_limit_bytes=EXCHANGE_VMEM
        ),
        name="exchange",
    )(abundance, spectra, support, panel_blocks)


def per_device(pix_count, eb_count, abundance, spectra, support, panel_blocks):
    rows, cols = abundance.shape
    bands = spectra.shape[1]
    support = support.T
    args = (abundance, spectra, support, panel_blocks)
    if eb_count == 4 and 1 < pix_count and PANEL % (SUB * pix_count) == 0 and rows % (4 * TILE_ROWS) == 0:
        panels, grams, inverse = sums_by_copies(pix_count, *args)
    else:
        panels, grams, inverse = sums_by_collectives(*args)
    params = pltpu.CompilerParams(vmem_limit_bytes=EXCHANGE_VMEM)
    trailing, residual, coefficients = pl.pallas_call(
        update_kernel,
        out_shape=(
            jax.ShapeDtypeStruct((rows, cols), jnp.float32),
            jax.ShapeDtypeStruct((rows, bands), jnp.float32),
            jax.ShapeDtypeStruct((WIDTH, bands), jnp.float32),
        ),
        in_specs=[HBM, HBM, SMEM, HBM, VMEM, VMEM],
        out_specs=(HBM, HBM, VMEM),
        scratch_shapes=[
            pltpu.VMEM((rows, cols), jnp.float32),
            pltpu.VMEM((rows, bands), jnp.float32),
            pltpu.VMEM((rows, WIDTH), jnp.float32),
            pltpu.VMEM((rows, cols), jnp.float32),
            pltpu.VMEM((rows, bands), jnp.float32),
            pltpu.SemaphoreType.DMA((3,)),
            pltpu.SemaphoreType.DMA((rows // TILE_ROWS,)),
            pltpu.SemaphoreType.DMA((rows // TILE_ROWS,)),
        ],
        compiler_params=params,
        name="update",
    )(abundance, spectra, support, panels, grams, inverse)
    return trailing, residual, coefficients.reshape(NPANELS, PANEL, bands)


def solution(mesh):
    placed = (P("pix", "eb"), P("pix", "eb"), P("pix", "eb"), P())
    return jax.shard_map(
        functools.partial(per_device, mesh.shape["pix"], mesh.shape["eb"]),
        mesh=mesh,
        in_specs=placed,
        out_specs=(P("pix", "eb"), P("pix", "eb"), P(None, None, "eb")),
        check_vma=False,
    )
```

```python
import functools

import jax
import jax.numpy as jnp
from jax import lax
from jax.experimental import pallas as pl
from jax.experimental.pallas import tpu as pltpu
from jax.sharding import PartitionSpec as P

PANEL = 64
TILE_ROWS = 128
NPANELS = 2
WIDTH = PANEL * NPANELS
SUB = 8
VMEM_LIMIT = 48 * 1024 * 1024
EXCHANGE_VMEM = 64 * 1024 * 1024 - 512 * 1024


def product(left, right):
    return jnp.dot(left, right, precision=lax.Precision.HIGHEST, preferred_element_type=jnp.float32)


def product_t(left, right):
    return lax.dot_general(
        left,
        right,
        (((0,), (0,)), ((), ())),
        precision=lax.Precision.HIGHEST,
        preferred_element_type=jnp.float32,
    )


def split(values):
    high = values.astype(jnp.bfloat16)
    return high, (values - high.astype(jnp.float32)).astype(jnp.bfloat16)


def plain(left, right):
    return jnp.dot(left, right, preferred_element_type=jnp.float32)


def product_nt(left, right):
    return lax.dot_general(
        left,
        right,
        (((1,), (1,)), ((), ())),
        precision=lax.Precision.HIGHEST,
        preferred_element_type=jnp.float32,
    )


def support_row(support_ref, tile, cols):
    lane = lax.broadcasted_iota(jnp.int32, (1, cols), 1)
    row = jnp.zeros((1, cols), jnp.float32)
    for block in range(cols // PANEL):
        value = support_ref[block, tile].astype(jnp.float32)
        row = jnp.where((lane >= block * PANEL) & (lane < (block + 1) * PANEL), value, row)
    return row


def inverse_factor(gram):
    shape = (SUB, WIDTH)
    count = PANEL // SUB
    sublane = lax.broadcasted_iota(jnp.int32, shape, 0)
    lane = lax.broadcasted_iota(jnp.int32, shape, 1)
    pad = jnp.concatenate([gram, jnp.zeros_like(gram)], axis=1)
    tiles = [
        pad[i * SUB : (i + 1) * SUB, :] + jnp.where(lane == sublane + (PANEL + i * SUB), 1.0, 0.0)
        for i in range(count)
    ]
    for block in range(count):
        low = block * SUB

        def spread(tile):
            return [jnp.broadcast_to(tile[:, low + j : low + j + 1], shape) for j in range(SUB)]

        rows = tiles[block]
        columns = spread(rows)
        below = {r: spread(tiles[r]) for r in range(block + 1, count)}
        entry = {
            (i, j): jnp.broadcast_to(columns[j][i : i + 1, :], shape)
            for j in range(SUB)
            for i in range(j, SUB)
        }
        g = [jnp.broadcast_to(rows[i : i + 1, :], shape) for i in range(SUB)]
        upper = rows
        for j in range(SUB):
            scale = lax.rsqrt(entry[j, j])
            for i in range(j + 1, SUB):
                entry[i, j] = entry[i, j] * scale
            g[j] = g[j] * scale
            for i in range(j + 1, SUB):
                for k in range(j + 1, i + 1):
                    entry[i, k] = entry[i, k] - entry[i, j] * entry[k, j]
                g[i] = g[i] - entry[i, j] * g[j]
            upper = jnp.where(sublane == j, g[j], upper)
            for r, column in below.items():
                column[j] = column[j] * scale
                for k in range(j + 1, SUB):
                    column[k] = column[k] - column[j] * entry[k, j]
                tiles[r] = tiles[r] - column[j] * g[j]
        tiles[block] = upper
    return jnp.concatenate(tiles, axis=0)[:, PANEL:]


def second_factor(inverse0, grams1, inverse_ref):
    coupling = product_nt(grams1[:, :PANEL], inverse0)
    remainder = grams1[:, PANEL:] - product_nt(coupling, coupling)
    carried = product(coupling, inverse0)
    inverse_ref[:PANEL, :] = jnp.concatenate([inverse0, jnp.zeros_like(inverse0)], axis=1)
    inverse1 = inverse_factor(remainder)
    inverse_ref[PANEL:, :] = jnp.concatenate([-product(inverse1, carried), inverse1], axis=1)


def gram_kernel(x_ref, y_ref, support_ref, c_ref, out_ref):
    rows, cols = x_ref.shape
    total = None
    for tile in range(rows // TILE_ROWS):
        panel = c_ref[tile_span(tile), :]
        masked = masked_tile(x_ref, support_ref, tile)
        joined = jnp.concatenate([masked, y_ref[tile_span(tile), :], panel], axis=1)
        part = product_t(panel, joined)
        total = part if total is None else total + part
    out_ref[...] = total


def factor_kernel(gram_ref, inverse_ref):
    inverse0 = inverse_factor(gram_ref[:PANEL, :PANEL])
    second_factor(inverse0, gram_ref[PANEL:, :], inverse_ref)


def update_kernel(
    x_hbm,
    y_hbm,
    support_ref,
    c_hbm,
    m_hbm,
    inverse_hbm,
    trail_hbm,
    resid_hbm,
    coef_hbm,
    x_ref,
    y_ref,
    c_ref,
    m_ref,
    inverse_ref,
    coef,
    trail,
    resid,
    in_sem,
    trail_sem,
    resid_sem,
    coef_sem,
):
    rows, cols = x_ref.shape
    pairs = [(inverse_hbm, inverse_ref), (m_hbm, m_ref), (c_hbm, c_ref), (x_hbm, x_ref), (y_hbm, y_ref)]
    loads = [pltpu.make_async_copy(src, dst, in_sem.at[index]) for index, (src, dst) in enumerate(pairs)]
    for copy in loads:
        copy.start()
    for copy in loads[:2]:
        copy.wait()
    inverse = inverse_ref[...]
    share = m_ref.shape[1] // NPANELS
    sums = jnp.concatenate(
        [m_ref[p, i * share : (i + 1) * share, :] for i in range(NPANELS) for p in range(m_ref.shape[0])], axis=0
    )
    proj = product(inverse, sums)
    coef[...] = proj[:, cols:]
    stores = [pltpu.make_async_copy(coef, coef_hbm, coef_sem)]
    stores[0].start()
    high, low = split(product_t(inverse, proj))
    weights = jnp.concatenate([high, high, low], axis=0)
    for copy in loads[2:]:
        copy.wait()
    for tile in range(rows // TILE_ROWS):
        span = pl.ds(tile * TILE_ROWS, TILE_ROWS)
        high, low = split(c_ref[span, :])
        change = plain(jnp.concatenate([high, low, high], axis=1), weights)
        trail[span, :] = masked_tile(x_ref, support_ref, tile) - change[:, :cols]
        resid[span, :] = y_ref[span, :] - change[:, cols:]
        stores.append(pltpu.make_async_copy(trail.at[span, :], trail_hbm.at[span, :], trail_sem.at[tile]))
        stores.append(pltpu.make_async_copy(resid.at[span, :], resid_hbm.at[span, :], resid_sem.at[tile]))
        stores[-2].start()
        stores[-1].start()
    for copy in stores:
        copy.wait()


def tile_span(tile):
    start = tile * TILE_ROWS
    return pl.ds(start if isinstance(start, int) else pl.multiple_of(start, TILE_ROWS), TILE_ROWS)


def masked_tile(x_ref, support_ref, tile):
    span = tile_span(tile)
    return x_ref[span, :] * support_row(support_ref, tile, x_ref.shape[1])


def own_panel_pair(x_ref, support_ref, blocks_ref, holder, tile):
    blocks_here = x_ref.shape[1] // PANEL
    left = lax.broadcasted_iota(jnp.int32, (1, WIDTH), 1) < PANEL
    totals = [jnp.zeros((TILE_ROWS, WIDTH), jnp.float32) for _ in range(NPANELS)]
    for place in range(2):
        for pair in range(blocks_here // 2):
            values = x_ref[tile_span(tile + place), pair * WIDTH : (pair + 1) * WIDTH]
            turned = pltpu.roll(values, PANEL, 1)
            for half in range(2):
                local = pair * 2 + half
                keep = support_ref[local, tile + place].astype(jnp.float32)
                source = values if half == place else turned
                for index in range(NPANELS):
                    factor = jnp.where(blocks_ref[index] == holder * blocks_here + local, keep, 0.0)
                    lanes = jnp.where(left, factor, 0.0) if place == 0 else jnp.where(left, 0.0, factor)
                    totals[index] = totals[index] + source * lanes
    return totals


def exchange_kernel(
    pix_count,
    x_hbm,
    y_hbm,
    support_ref,
    blocks_ref,
    c_hbm,
    m_ref,
    inverse_ref,
    x_ref,
    y_ref,
    c_ref,
    own,
    first_in,
    chip_sum,
    second_in,
    full,
    gram0_part,
    gram0,
    gram0_slots,
    gram1_part,
    gram1,
    gram1_slots,
    m0_part,
    m0_slots,
    m1_part,
    m1_slots,
    xy_high,
    xy_low,
    in_sem,
    out_sem,
    send1,
    recv1,
    send2,
    recv2,
    send3,
    recv3,
    gram0_sems,
    gram1_sems,
    m0_sems,
    m1_sems,
    gather_sems,
    near0_sems,
    near1_sems,
):
    rows, cols = x_ref.shape
    half = rows // 2
    chunks = half // (2 * TILE_ROWS)
    pix = lax.axis_index("pix")
    eb = lax.axis_index("eb")
    core = eb % 2
    other_core = 1 - core
    beside = eb + 1 - 2 * core
    across = (eb + 2) % 4
    others = [(pix + d) % pix_count for d in range(1, pix_count)]

    def side_of(ref, side):
        return ref.at[pl.ds(pl.multiple_of(side * half, TILE_ROWS), half), :]

    loads = []
    for index, (src, dst) in enumerate(
        [
            (side_of(x_hbm, other_core), side_of(x_ref, other_core)),
            (side_of(x_hbm, core), side_of(x_ref, core)),
            (y_hbm, y_ref),
        ]
    ):
        loads.append(pltpu.make_async_copy(src, dst, in_sem.at[index]))
        loads[-1].start()

    barrier = pltpu.get_barrier_semaphore()
    near = [(pix, (eb + d) % 4) for d in range(1, 4)]
    for target in near + [(other, eb) for other in others]:
        pl.semaphore_signal(barrier, inc=1, device_id=target, device_id_type=pl.DeviceIdType.MESH)

    started = []

    def send(src, dst, send_sem, recv_sem, target):
        copy = pltpu.make_async_remote_copy(
            src_ref=src,
            dst_ref=dst,
            send_sem=send_sem,
            recv_sem=recv_sem,
            device_id=target,
            device_id_type=pl.DeviceIdType.MESH,
        )
        copy.start()
        started.append(copy)
        return copy

    def prepare(side, chunk):
        pair = side * chunks + chunk
        for index, values in enumerate(own_panel_pair(x_ref, support_ref, blocks_ref, eb, pair * 2)):
            own[index, pair] = values

    def pair_span(pair):
        return pl.ds(pl.multiple_of(pair * (2 * TILE_ROWS), 2 * TILE_ROWS), 2 * TILE_ROWS)

    def unpack(index, pair):
        packed = full[index, pair]
        lanes = slice(index * PANEL, (index + 1) * PANEL)
        c_ref[tile_span(pair * 2), lanes] = packed[:, :PANEL]
        c_ref[tile_span(pair * 2 + 1), lanes] = packed[:, PANEL:]

    def gram_of(index):
        return product_t(c_ref[:, index * PANEL : (index + 1) * PANEL], c_ref[...])

    def add_products(index, pair, part, first):
        panel = c_ref[pair_span(pair), index * PANEL : (index + 1) * PANEL]
        high, low = split(panel.T)
        both = plain(jnp.concatenate([high, low], axis=0), xy_high[pair_span(pair), :])
        value = both[:PANEL] + both[PANEL:] + plain(high, xy_low[pair_span(pair), :])
        part[...] = value if first else part[...] + value

    share = PANEL // pix_count
    mine = pl.ds(pl.multiple_of(pix * share, share), share)

    def scatter(part, landing, sems):
        copies = []
        for index, other in enumerate(others):
            rows_there = pl.ds(pl.multiple_of(other * share, share), share)
            copies.append(
                send(part.at[rows_there, :], landing.at[index], sems.at[0, index], sems.at[1, index], (other, eb))
            )
        return copies

    def add_up(part, landing, copies):
        total = part[mine, :]
        for index in range(pix_count - 1):
            copies[index].wait_recv()
            total = total + landing[index]
        return total

    def gather(block, sems, place):
        return [
            send(block, block, sems.at[place, index], sems.at[place + 1, index], (other, eb))
            for index, other in enumerate(others)
        ]

    quarter = PANEL // 4
    here = pl.ds(pl.multiple_of(eb * quarter, quarter), quarter)

    def spread_gram(part, landing, sems):
        return [
            send(part.at[here, :], landing.at[index], sems.at[0, index], sems.at[1, index], (other, eb))
            for index, other in enumerate(others)
        ]

    def share_gram(part, landing, gram, copies, sems):
        total = part[here, :]
        for index in range(pix_count - 1):
            copies[index].wait_recv()
            total = total + landing[index]
        gram[here, :] = total
        return [
            send(gram.at[here, :], gram.at[here, :], sems.at[0, index], sems.at[1, index], target)
            for index, target in enumerate(near)
        ]

    def arrive(index, part):
        copies3 = []
        for chunk in range(chunks):
            copies2[index][chunk].wait_recv()
            pair = core * chunks + chunk
            full[index, pair] = chip_sum[index, chunk] + second_in[index, chunk]
            copies3.append(
                send(
                    full.at[index, pair],
                    full.at[index, pair],
                    send3.at[index, chunk],
                    recv3.at[index, chunk],
                    (pix, beside),
                )
            )
            unpack(index, pair)
            add_products(index, pair, part, chunk == 0)
        for chunk in range(chunks):
            copies3[chunk].wait_recv()
            pair = other_core * chunks + chunk
            unpack(index, pair)
            add_products(index, pair, part, False)

    c_ref[...] = jnp.zeros_like(c_ref)
    loads[0].wait()
    for chunk in range(chunks):
        prepare(other_core, chunk)
    pl.semaphore_wait(barrier, pix_count + 2)
    copies1 = [
        [
            send(
                own.at[index, other_core * chunks + chunk],
                first_in.at[index, chunk],
                send1.at[index, chunk],
                recv1.at[index, chunk],
                (pix, beside),
            )
            for chunk in range(chunks)
        ]
        for index in range(NPANELS)
    ]
    loads[1].wait()
    for chunk in range(chunks):
        prepare(core, chunk)
    copies2 = []
    for index in range(NPANELS):
        copies2.append([])
        for chunk in range(chunks):
            copies1[index][chunk].wait_recv()
            chip_sum[index, chunk] = own[index, core * chunks + chunk] + first_in[index, chunk]
            copies2[index].append(
                send(
                    chip_sum.at[index, chunk],
                    second_in.at[index, chunk],
                    send2.at[index, chunk],
                    recv2.at[index, chunk],
                    (pix, across),
                )
            )
    loads[2].wait()
    for tile in range(rows // TILE_ROWS):
        for values, lanes in [
            (masked_tile(x_ref, support_ref, tile), slice(0, cols)),
            (y_ref[tile_span(tile), :], slice(cols, None)),
        ]:
            high, low = split(values)
            xy_high[tile_span(tile), lanes] = high
            xy_low[tile_span(tile), lanes] = low

    low_rows = pl.ds(0, share)
    high_rows = pl.ds(share, share)

    arrive(0, m0_part)
    m0_copies = scatter(m0_part, m0_slots, m0_sems)
    gram0_part[...] = gram_of(0)
    gram0_copies = spread_gram(gram0_part, gram0_slots, gram0_sems)

    arrive(1, m1_part)
    m1_copies = scatter(m1_part, m1_slots, m1_sems)
    gram0_near = share_gram(gram0_part, gram0_slots, gram0, gram0_copies, near0_sems)
    gram1_part[...] = gram_of(1)
    gram1_copies = spread_gram(gram1_part, gram1_slots, gram1_sems)
    keep_c = pltpu.make_async_copy(c_ref, c_hbm, out_sem)
    keep_c.start()
    m_ref[pix, low_rows, :] = add_up(m0_part, m0_slots, m0_copies)
    m0_gather = gather(m_ref.at[pix, low_rows, :], gather_sems, 0)

    for copy in gram0_near:
        copy.wait_recv()
    inverse0 = inverse_factor(gram0[:, :PANEL])
    gram1_near = share_gram(gram1_part, gram1_slots, gram1, gram1_copies, near1_sems)
    m_ref[pix, high_rows, :] = add_up(m1_part, m1_slots, m1_copies)
    m1_gather = gather(m_ref.at[pix, high_rows, :], gather_sems, 2)
    for copy in gram1_near:
        copy.wait_recv()
    second_factor(inverse0, gram1[...], inverse_ref)
    for copy in m0_gather + m1_gather:
        copy.wait_recv()
    for copy in started:
        copy.wait_send()
    keep_c.wait()


VMEM = pl.BlockSpec(memory_space=pltpu.VMEM)
SMEM = pl.BlockSpec(memory_space=pltpu.SMEM)
HBM = pl.BlockSpec(memory_space=pltpu.HBM)


def own_panels(abundance, support, panel_blocks, holder):
    blocks_here = abundance.shape[1] // PANEL
    parts = []
    for index in range(NPANELS):
        block = panel_blocks[index]
        local = block % blocks_here
        panel = lax.dynamic_slice_in_dim(abundance, local * PANEL, PANEL, 1)
        keep = lax.dynamic_slice_in_dim(support, local, 1, 1).astype(jnp.float32)
        keep = jnp.where(block // blocks_here == holder, keep, 0.0)
        parts.append((panel.reshape(-1, TILE_ROWS, PANEL) * keep[:, :, None]).reshape(-1, PANEL))
    return jnp.concatenate(parts, axis=1)


def sums_by_collectives(abundance, spectra, support, panel_blocks):
    cols = abundance.shape[1]
    bands = spectra.shape[1]
    own = own_panels(abundance, support.T, panel_blocks, lax.axis_index("eb"))
    panels = lax.psum(own, "eb")
    grams = pl.pallas_call(
        gram_kernel,
        out_shape=jax.ShapeDtypeStruct((WIDTH, cols + bands + WIDTH), jnp.float32),
        in_specs=[VMEM, VMEM, SMEM, VMEM],
        out_specs=VMEM,
        compiler_params=pltpu.CompilerParams(vmem_limit_bytes=VMEM_LIMIT),
        name="gram",
    )(abundance, spectra, support, panels)
    grams = lax.psum(grams, "pix")
    inverse = pl.pallas_call(
        factor_kernel,
        out_shape=jax.ShapeDtypeStruct((WIDTH, WIDTH), jnp.float32),
        in_specs=[VMEM],
        out_specs=VMEM,
        compiler_params=pltpu.CompilerParams(vmem_limit_bytes=VMEM_LIMIT),
        name="factor",
    )(grams[:, cols + bands :])
    return panels, grams[:, : cols + bands].reshape(1, WIDTH, cols + bands), inverse


def sums_by_copies(pix_count, abundance, spectra, support, panel_blocks):
    rows, cols = abundance.shape
    width = cols + spectra.shape[1]
    chunks = rows // (4 * TILE_ROWS)
    share = PANEL // pix_count
    away = pix_count - 1
    dma = pltpu.SemaphoreType.DMA

    def buffer(*shape):
        return pltpu.VMEM(shape, jnp.float32)

    return pl.pallas_call(
        functools.partial(exchange_kernel, pix_count),
        out_shape=(
            jax.ShapeDtypeStruct((rows, WIDTH), jnp.float32),
            jax.ShapeDtypeStruct((pix_count, NPANELS * share, width), jnp.float32),
            jax.ShapeDtypeStruct((WIDTH, WIDTH), jnp.float32),
        ),
        in_specs=[HBM, HBM, SMEM, SMEM],
        out_specs=(HBM, VMEM, VMEM),
        scratch_shapes=[
            buffer(*abundance.shape),
            buffer(*spectra.shape),
            buffer(rows, WIDTH),
            buffer(NPANELS, 2 * chunks, TILE_ROWS, WIDTH),
            buffer(NPANELS, chunks, TILE_ROWS, WIDTH),
            buffer(NPANELS, chunks, TILE_ROWS, WIDTH),
            buffer(NPANELS, chunks, TILE_ROWS, WIDTH),
            buffer(NPANELS, 2 * chunks, TILE_ROWS, WIDTH),
            buffer(PANEL, WIDTH),
            buffer(PANEL, WIDTH),
            buffer(away, PANEL // 4, WIDTH),
            buffer(PANEL, WIDTH),
            buffer(PANEL, WIDTH),
            buffer(away, PANEL // 4, WIDTH),
            buffer(PANEL, width),
            buffer(away, share, width),
            buffer(PANEL, width),
            buffer(away, share, width),
            pltpu.VMEM((rows, width), jnp.bfloat16),
            pltpu.VMEM((rows, width), jnp.bfloat16),
            dma((3,)),
            dma,
        ]
        + [dma((NPANELS, chunks))] * 6
        + [dma((2, away))] * 4
        + [dma((4, away)), dma((2, 3)), dma((2, 3))],
        compiler_params=pltpu.CompilerParams(
            collective_id=0, has_side_effects=True, vmem_limit_bytes=EXCHANGE_VMEM
        ),
        name="exchange",
    )(abundance, spectra, support, panel_blocks)


def per_device(pix_count, eb_count, abundance, spectra, support, panel_blocks):
    rows, cols = abundance.shape
    bands = spectra.shape[1]
    support = support.T
    args = (abundance, spectra, support, panel_blocks)
    if eb_count == 4 and 1 < pix_count and PANEL % (SUB * pix_count) == 0 and rows % (4 * TILE_ROWS) == 0:
        panels, grams, inverse = sums_by_copies(pix_count, *args)
    else:
        panels, grams, inverse = sums_by_collectives(*args)
    params = pltpu.CompilerParams(vmem_limit_bytes=EXCHANGE_VMEM)
    trailing, residual, coefficients = pl.pallas_call(
        update_kernel,
        out_shape=(
            jax.ShapeDtypeStruct((rows, cols), jnp.float32),
            jax.ShapeDtypeStruct((rows, bands), jnp.float32),
            jax.ShapeDtypeStruct((WIDTH, bands), jnp.float32),
        ),
        in_specs=[HBM, HBM, SMEM, HBM, HBM, HBM],
        out_specs=(HBM, HBM, HBM),
        scratch_shapes=[
            pltpu.VMEM((rows, cols), jnp.float32),
            pltpu.VMEM((rows, bands), jnp.float32),
            pltpu.VMEM((rows, WIDTH), jnp.float32),
            pltpu.VMEM(grams.shape, jnp.float32),
            pltpu.VMEM((WIDTH, WIDTH), jnp.float32),
            pltpu.VMEM((WIDTH, bands), jnp.float32),
            pltpu.VMEM((rows, cols), jnp.float32),
            pltpu.VMEM((rows, bands), jnp.float32),
            pltpu.SemaphoreType.DMA((5,)),
            pltpu.SemaphoreType.DMA((rows // TILE_ROWS,)),
            pltpu.SemaphoreType.DMA((rows // TILE_ROWS,)),
            pltpu.SemaphoreType.DMA,
        ],
        compiler_params=params,
        name="update",
    )(abundance, spectra, support, panels, grams, inverse)
    return trailing, residual, coefficients.reshape(NPANELS, PANEL, bands)


def solution(mesh):
    placed = (P("pix", "eb"), P("pix", "eb"), P("pix", "eb"), P())
    return jax.shard_map(
        functools.partial(per_device, mesh.shape["pix"], mesh.shape["eb"]),
        mesh=mesh,
        in_specs=placed,
        out_specs=(P("pix", "eb"), P("pix", "eb"), P(None, None, "eb")),
        check_vma=False,
    )
```

```python
import functools

import jax
import jax.numpy as jnp
from jax import lax
from jax.experimental import pallas as pl
from jax.experimental.pallas import tpu as pltpu
from jax.sharding import PartitionSpec as P

PANEL = 64
TILE_ROWS = 128
NPANELS = 2
WIDTH = PANEL * NPANELS
SUB = 8
VMEM_LIMIT = 48 * 1024 * 1024
EXCHANGE_VMEM = 64 * 1024 * 1024 - 512 * 1024


def product(left, right):
    return jnp.dot(left, right, precision=lax.Precision.HIGHEST, preferred_element_type=jnp.float32)


def product_t(left, right):
    return lax.dot_general(
        left,
        right,
        (((0,), (0,)), ((), ())),
        precision=lax.Precision.HIGHEST,
        preferred_element_type=jnp.float32,
    )


def split(values):
    high = values.astype(jnp.bfloat16)
    return high, (values - high.astype(jnp.float32)).astype(jnp.bfloat16)


def plain(left, right):
    return jnp.dot(left, right, preferred_element_type=jnp.float32)


def product_nt(left, right):
    return lax.dot_general(
        left,
        right,
        (((1,), (1,)), ((), ())),
        precision=lax.Precision.HIGHEST,
        preferred_element_type=jnp.float32,
    )


def support_row(support_ref, tile, cols):
    lane = lax.broadcasted_iota(jnp.int32, (1, cols), 1)
    row = jnp.zeros((1, cols), jnp.float32)
    for block in range(cols // PANEL):
        value = support_ref[block, tile].astype(jnp.float32)
        row = jnp.where((lane >= block * PANEL) & (lane < (block + 1) * PANEL), value, row)
    return row


def inverse_factor(gram):
    shape = (SUB, WIDTH)
    count = PANEL // SUB
    sublane = lax.broadcasted_iota(jnp.int32, shape, 0)
    lane = lax.broadcasted_iota(jnp.int32, shape, 1)
    pad = jnp.concatenate([gram, jnp.zeros_like(gram)], axis=1)
    tiles = [
        pad[i * SUB : (i + 1) * SUB, :] + jnp.where(lane == sublane + (PANEL + i * SUB), 1.0, 0.0)
        for i in range(count)
    ]
    for block in range(count):
        low = block * SUB

        def spread(tile):
            return [jnp.broadcast_to(tile[:, low + j : low + j + 1], shape) for j in range(SUB)]

        rows = tiles[block]
        columns = spread(rows)
        below = {r: spread(tiles[r]) for r in range(block + 1, count)}
        entry = {
            (i, j): jnp.broadcast_to(columns[j][i : i + 1, :], shape)
            for j in range(SUB)
            for i in range(j, SUB)
        }
        g = [jnp.broadcast_to(rows[i : i + 1, :], shape) for i in range(SUB)]
        upper = rows
        for j in range(SUB):
            scale = lax.rsqrt(entry[j, j])
            for i in range(j + 1, SUB):
                entry[i, j] = entry[i, j] * scale
            g[j] = g[j] * scale
            for i in range(j + 1, SUB):
                for k in range(j + 1, i + 1):
                    entry[i, k] = entry[i, k] - entry[i, j] * entry[k, j]
                g[i] = g[i] - entry[i, j] * g[j]
            upper = jnp.where(sublane == j, g[j], upper)
            for r, column in below.items():
                column[j] = column[j] * scale
                for k in range(j + 1, SUB):
                    column[k] = column[k] - column[j] * entry[k, j]
                tiles[r] = tiles[r] - column[j] * g[j]
        tiles[block] = upper
    return jnp.concatenate(tiles, axis=0)[:, PANEL:]


def second_factor(inverse0, grams1, inverse_ref):
    coupling = product_nt(grams1[:, :PANEL], inverse0)
    remainder = grams1[:, PANEL:] - product_nt(coupling, coupling)
    carried = product(coupling, inverse0)
    inverse_ref[:PANEL, :] = jnp.concatenate([inverse0, jnp.zeros_like(inverse0)], axis=1)
    inverse1 = inverse_factor(remainder)
    inverse_ref[PANEL:, :] = jnp.concatenate([-product(inverse1, carried), inverse1], axis=1)


def gram_kernel(x_ref, y_ref, support_ref, c_ref, out_ref):
    rows, cols = x_ref.shape
    total = None
    for tile in range(rows // TILE_ROWS):
        panel = c_ref[tile_span(tile), :]
        masked = masked_tile(x_ref, support_ref, tile)
        joined = jnp.concatenate([masked, y_ref[tile_span(tile), :], panel], axis=1)
        part = product_t(panel, joined)
        total = part if total is None else total + part
    out_ref[...] = total


def factor_kernel(gram_ref, inverse_ref):
    inverse0 = inverse_factor(gram_ref[:PANEL, :PANEL])
    second_factor(inverse0, gram_ref[PANEL:, :], inverse_ref)


def update_kernel(
    x_hbm,
    y_hbm,
    support_ref,
    c_hbm,
    m_hbm,
    inverse_hbm,
    trail_hbm,
    resid_hbm,
    coef_hbm,
    x_ref,
    y_ref,
    c_ref,
    m_ref,
    inverse_ref,
    coef,
    trail,
    resid,
    in_sem,
    trail_sem,
    resid_sem,
    coef_sem,
):
    rows, cols = x_ref.shape
    pairs = [(inverse_hbm, inverse_ref), (m_hbm, m_ref), (c_hbm, c_ref), (x_hbm, x_ref), (y_hbm, y_ref)]
    loads = [pltpu.make_async_copy(src, dst, in_sem.at[index]) for index, (src, dst) in enumerate(pairs)]
    for copy in loads:
        copy.start()
    for copy in loads[:2]:
        copy.wait()
    inverse = inverse_ref[...]
    share = m_ref.shape[1] // NPANELS
    sums = jnp.concatenate(
        [m_ref[p, i * share : (i + 1) * share, :] for i in range(NPANELS) for p in range(m_ref.shape[0])], axis=0
    )
    proj = product(inverse, sums)
    coef[...] = proj[:, cols:]
    stores = [pltpu.make_async_copy(coef, coef_hbm, coef_sem)]
    stores[0].start()
    high, low = split(product_t(inverse, proj))
    weights = jnp.concatenate([high, high, low], axis=0)
    for copy in loads[2:]:
        copy.wait()
    for tile in range(rows // TILE_ROWS):
        span = pl.ds(tile * TILE_ROWS, TILE_ROWS)
        high, low = split(c_ref[span, :])
        change = plain(jnp.concatenate([high, low, high], axis=1), weights)
        trail[span, :] = masked_tile(x_ref, support_ref, tile) - change[:, :cols]
        resid[span, :] = y_ref[span, :] - change[:, cols:]
        stores.append(pltpu.make_async_copy(trail.at[span, :], trail_hbm.at[span, :], trail_sem.at[tile]))
        stores.append(pltpu.make_async_copy(resid.at[span, :], resid_hbm.at[span, :], resid_sem.at[tile]))
        stores[-2].start()
        stores[-1].start()
    for copy in stores:
        copy.wait()


def tile_span(tile):
    start = tile * TILE_ROWS
    return pl.ds(start if isinstance(start, int) else pl.multiple_of(start, TILE_ROWS), TILE_ROWS)


def masked_tile(x_ref, support_ref, tile):
    span = tile_span(tile)
    return x_ref[span, :] * support_row(support_ref, tile, x_ref.shape[1])


def own_panel_pair(x_ref, support_ref, blocks_ref, holder, tile):
    blocks_here = x_ref.shape[1] // PANEL
    left = lax.broadcasted_iota(jnp.int32, (1, WIDTH), 1) < PANEL
    totals = [jnp.zeros((TILE_ROWS, WIDTH), jnp.float32) for _ in range(NPANELS)]
    for place in range(2):
        for pair in range(blocks_here // 2):
            values = x_ref[tile_span(tile + place), pair * WIDTH : (pair + 1) * WIDTH]
            turned = pltpu.roll(values, PANEL, 1)
            for half in range(2):
                local = pair * 2 + half
                keep = support_ref[local, tile + place].astype(jnp.float32)
                source = values if half == place else turned
                for index in range(NPANELS):
                    factor = jnp.where(blocks_ref[index] == holder * blocks_here + local, keep, 0.0)
                    lanes = jnp.where(left, factor, 0.0) if place == 0 else jnp.where(left, 0.0, factor)
                    totals[index] = totals[index] + source * lanes
    return totals


def exchange_kernel(
    pix_count,
    x_hbm,
    y_hbm,
    support_hbm,
    blocks_hbm,
    c_hbm,
    m_ref,
    inverse_ref,
    x_ref,
    y_ref,
    support_ref,
    blocks_ref,
    c_ref,
    own,
    first_in,
    chip_sum,
    second_in,
    full,
    gram0_part,
    gram0,
    gram0_slots,
    gram1_part,
    gram1,
    gram1_slots,
    m0_part,
    m0_slots,
    m1_part,
    m1_slots,
    xy_high,
    xy_low,
    in_sem,
    out_sem,
    send1,
    recv1,
    send2,
    recv2,
    send3,
    recv3,
    gram0_sems,
    gram1_sems,
    m0_sems,
    m1_sems,
    gather_sems,
    near0_sems,
    near1_sems,
):
    rows, cols = x_ref.shape
    half = rows // 2
    chunks = half // (2 * TILE_ROWS)
    pix = lax.axis_index("pix")
    eb = lax.axis_index("eb")
    core = eb % 2
    other_core = 1 - core
    beside = eb + 1 - 2 * core
    across = (eb + 2) % 4
    others = [(pix + d) % pix_count for d in range(1, pix_count)]

    def side_of(ref, side):
        return ref.at[pl.ds(pl.multiple_of(side * half, TILE_ROWS), half), :]

    loads = []
    for index, (src, dst) in enumerate(
        [
            (side_of(x_hbm, other_core), side_of(x_ref, other_core)),
            (side_of(x_hbm, core), side_of(x_ref, core)),
            (y_hbm, y_ref),
            (support_hbm, support_ref),
            (blocks_hbm, blocks_ref),
        ]
    ):
        loads.append(pltpu.make_async_copy(src, dst, in_sem.at[index]))
        loads[-1].start()

    barrier = pltpu.get_barrier_semaphore()
    near = [(pix, (eb + d) % 4) for d in range(1, 4)]
    for target in near + [(other, eb) for other in others]:
        pl.semaphore_signal(barrier, inc=1, device_id=target, device_id_type=pl.DeviceIdType.MESH)

    started = []

    def send(src, dst, send_sem, recv_sem, target):
        copy = pltpu.make_async_remote_copy(
            src_ref=src,
            dst_ref=dst,
            send_sem=send_sem,
            recv_sem=recv_sem,
            device_id=target,
            device_id_type=pl.DeviceIdType.MESH,
        )
        copy.start()
        started.append(copy)
        return copy

    def prepare(side, chunk):
        pair = side * chunks + chunk
        for index, values in enumerate(own_panel_pair(x_ref, support_ref, blocks_ref, eb, pair * 2)):
            own[index, pair] = values

    def pair_span(pair):
        return pl.ds(pl.multiple_of(pair * (2 * TILE_ROWS), 2 * TILE_ROWS), 2 * TILE_ROWS)

    def unpack(index, pair):
        packed = full[index, pair]
        lanes = slice(index * PANEL, (index + 1) * PANEL)
        c_ref[tile_span(pair * 2), lanes] = packed[:, :PANEL]
        c_ref[tile_span(pair * 2 + 1), lanes] = packed[:, PANEL:]

    def gram_of(index):
        return product_t(c_ref[:, index * PANEL : (index + 1) * PANEL], c_ref[...])

    def add_products(index, pair, part, first):
        panel = c_ref[pair_span(pair), index * PANEL : (index + 1) * PANEL]
        high, low = split(panel.T)
        both = plain(jnp.concatenate([high, low], axis=0), xy_high[pair_span(pair), :])
        value = both[:PANEL] + both[PANEL:] + plain(high, xy_low[pair_span(pair), :])
        part[...] = value if first else part[...] + value

    share = PANEL // pix_count
    mine = pl.ds(pl.multiple_of(pix * share, share), share)

    def scatter(part, landing, sems):
        copies = []
        for index, other in enumerate(others):
            rows_there = pl.ds(pl.multiple_of(other * share, share), share)
            copies.append(
                send(part.at[rows_there, :], landing.at[index], sems.at[0, index], sems.at[1, index], (other, eb))
            )
        return copies

    def add_up(part, landing, copies):
        total = part[mine, :]
        for index in range(pix_count - 1):
            copies[index].wait_recv()
            total = total + landing[index]
        return total

    def gather(block, sems, place):
        return [
            send(block, block, sems.at[place, index], sems.at[place + 1, index], (other, eb))
            for index, other in enumerate(others)
        ]

    quarter = PANEL // 4
    here = pl.ds(pl.multiple_of(eb * quarter, quarter), quarter)

    def spread_gram(part, landing, sems):
        return [
            send(part.at[here, :], landing.at[index], sems.at[0, index], sems.at[1, index], (other, eb))
            for index, other in enumerate(others)
        ]

    def share_gram(part, landing, gram, copies, sems):
        total = part[here, :]
        for index in range(pix_count - 1):
            copies[index].wait_recv()
            total = total + landing[index]
        gram[here, :] = total
        return [
            send(gram.at[here, :], gram.at[here, :], sems.at[0, index], sems.at[1, index], target)
            for index, target in enumerate(near)
        ]

    def arrive(index, part):
        copies3 = []
        for chunk in range(chunks):
            copies2[index][chunk].wait_recv()
            pair = core * chunks + chunk
            full[index, pair] = chip_sum[index, chunk] + second_in[index, chunk]
            copies3.append(
                send(
                    full.at[index, pair],
                    full.at[index, pair],
                    send3.at[index, chunk],
                    recv3.at[index, chunk],
                    (pix, beside),
                )
            )
            unpack(index, pair)
            add_products(index, pair, part, chunk == 0)
        for chunk in range(chunks):
            copies3[chunk].wait_recv()
            pair = other_core * chunks + chunk
            unpack(index, pair)
            add_products(index, pair, part, False)

    c_ref[...] = jnp.zeros_like(c_ref)
    loads[3].wait()
    loads[4].wait()
    loads[0].wait()
    for chunk in range(chunks):
        prepare(other_core, chunk)
    pl.semaphore_wait(barrier, pix_count + 2)
    copies1 = [
        [
            send(
                own.at[index, other_core * chunks + chunk],
                first_in.at[index, chunk],
                send1.at[index, chunk],
                recv1.at[index, chunk],
                (pix, beside),
            )
            for chunk in range(chunks)
        ]
        for index in range(NPANELS)
    ]
    loads[1].wait()
    for chunk in range(chunks):
        prepare(core, chunk)
    copies2 = []
    for index in range(NPANELS):
        copies2.append([])
        for chunk in range(chunks):
            copies1[index][chunk].wait_recv()
            chip_sum[index, chunk] = own[index, core * chunks + chunk] + first_in[index, chunk]
            copies2[index].append(
                send(
                    chip_sum.at[index, chunk],
                    second_in.at[index, chunk],
                    send2.at[index, chunk],
                    recv2.at[index, chunk],
                    (pix, across),
                )
            )
    loads[2].wait()
    for tile in range(rows // TILE_ROWS):
        for values, lanes in [
            (masked_tile(x_ref, support_ref, tile), slice(0, cols)),
            (y_ref[tile_span(tile), :], slice(cols, None)),
        ]:
            high, low = split(values)
            xy_high[tile_span(tile), lanes] = high
            xy_low[tile_span(tile), lanes] = low

    low_rows = pl.ds(0, share)
    high_rows = pl.ds(share, share)

    arrive(0, m0_part)
    m0_copies = scatter(m0_part, m0_slots, m0_sems)
    gram0_part[...] = gram_of(0)
    gram0_copies = spread_gram(gram0_part, gram0_slots, gram0_sems)

    arrive(1, m1_part)
    m1_copies = scatter(m1_part, m1_slots, m1_sems)
    gram0_near = share_gram(gram0_part, gram0_slots, gram0, gram0_copies, near0_sems)
    gram1_part[...] = gram_of(1)
    gram1_copies = spread_gram(gram1_part, gram1_slots, gram1_sems)
    keep_c = pltpu.make_async_copy(c_ref, c_hbm, out_sem)
    keep_c.start()
    m_ref[pix, low_rows, :] = add_up(m0_part, m0_slots, m0_copies)
    m0_gather = gather(m_ref.at[pix, low_rows, :], gather_sems, 0)

    for copy in gram0_near:
        copy.wait_recv()
    inverse0 = inverse_factor(gram0[:, :PANEL])
    gram1_near = share_gram(gram1_part, gram1_slots, gram1, gram1_copies, near1_sems)
    m_ref[pix, high_rows, :] = add_up(m1_part, m1_slots, m1_copies)
    m1_gather = gather(m_ref.at[pix, high_rows, :], gather_sems, 2)
    for copy in gram1_near:
        copy.wait_recv()
    second_factor(inverse0, gram1[...], inverse_ref)
    for copy in started[: -len(m1_gather)]:
        copy.wait_send()
    keep_c.wait()
    for copy in m0_gather + m1_gather:
        copy.wait_recv()
    for copy in m1_gather:
        copy.wait_send()


VMEM = pl.BlockSpec(memory_space=pltpu.VMEM)
SMEM = pl.BlockSpec(memory_space=pltpu.SMEM)
HBM = pl.BlockSpec(memory_space=pltpu.HBM)


def own_panels(abundance, support, panel_blocks, holder):
    blocks_here = abundance.shape[1] // PANEL
    parts = []
    for index in range(NPANELS):
        block = panel_blocks[index]
        local = block % blocks_here
        panel = lax.dynamic_slice_in_dim(abundance, local * PANEL, PANEL, 1)
        keep = lax.dynamic_slice_in_dim(support, local, 1, 1).astype(jnp.float32)
        keep = jnp.where(block // blocks_here == holder, keep, 0.0)
        parts.append((panel.reshape(-1, TILE_ROWS, PANEL) * keep[:, :, None]).reshape(-1, PANEL))
    return jnp.concatenate(parts, axis=1)


def sums_by_collectives(abundance, spectra, support, panel_blocks):
    cols = abundance.shape[1]
    bands = spectra.shape[1]
    own = own_panels(abundance, support.T, panel_blocks, lax.axis_index("eb"))
    panels = lax.psum(own, "eb")
    grams = pl.pallas_call(
        gram_kernel,
        out_shape=jax.ShapeDtypeStruct((WIDTH, cols + bands + WIDTH), jnp.float32),
        in_specs=[VMEM, VMEM, SMEM, VMEM],
        out_specs=VMEM,
        compiler_params=pltpu.CompilerParams(vmem_limit_bytes=VMEM_LIMIT),
        name="gram",
    )(abundance, spectra, support, panels)
    grams = lax.psum(grams, "pix")
    inverse = pl.pallas_call(
        factor_kernel,
        out_shape=jax.ShapeDtypeStruct((WIDTH, WIDTH), jnp.float32),
        in_specs=[VMEM],
        out_specs=VMEM,
        compiler_params=pltpu.CompilerParams(vmem_limit_bytes=VMEM_LIMIT),
        name="factor",
    )(grams[:, cols + bands :])
    return panels, grams[:, : cols + bands].reshape(1, WIDTH, cols + bands), inverse


def sums_by_copies(pix_count, abundance, spectra, support, panel_blocks):
    rows, cols = abundance.shape
    width = cols + spectra.shape[1]
    chunks = rows // (4 * TILE_ROWS)
    share = PANEL // pix_count
    away = pix_count - 1
    dma = pltpu.SemaphoreType.DMA

    def buffer(*shape):
        return pltpu.VMEM(shape, jnp.float32)

    return pl.pallas_call(
        functools.partial(exchange_kernel, pix_count),
        out_shape=(
            jax.ShapeDtypeStruct((rows, WIDTH), jnp.float32),
            jax.ShapeDtypeStruct((pix_count, NPANELS * share, width), jnp.float32),
            jax.ShapeDtypeStruct((WIDTH, WIDTH), jnp.float32),
        ),
        in_specs=[HBM, HBM, HBM, HBM],
        out_specs=(HBM, VMEM, VMEM),
        scratch_shapes=[
            buffer(*abundance.shape),
            buffer(*spectra.shape),
            pltpu.SMEM(support.shape, jnp.int32),
            pltpu.SMEM(panel_blocks.shape, jnp.int32),
            buffer(rows, WIDTH),
            buffer(NPANELS, 2 * chunks, TILE_ROWS, WIDTH),
            buffer(NPANELS, chunks, TILE_ROWS, WIDTH),
            buffer(NPANELS, chunks, TILE_ROWS, WIDTH),
            buffer(NPANELS, chunks, TILE_ROWS, WIDTH),
            buffer(NPANELS, 2 * chunks, TILE_ROWS, WIDTH),
            buffer(PANEL, WIDTH),
            buffer(PANEL, WIDTH),
            buffer(away, PANEL // 4, WIDTH),
            buffer(PANEL, WIDTH),
            buffer(PANEL, WIDTH),
            buffer(away, PANEL // 4, WIDTH),
            buffer(PANEL, width),
            buffer(away, share, width),
            buffer(PANEL, width),
            buffer(away, share, width),
            pltpu.VMEM((rows, width), jnp.bfloat16),
            pltpu.VMEM((rows, width), jnp.bfloat16),
            dma((5,)),
            dma,
        ]
        + [dma((NPANELS, chunks))] * 6
        + [dma((2, away))] * 4
        + [dma((4, away)), dma((2, 3)), dma((2, 3))],
        compiler_params=pltpu.CompilerParams(
            collective_id=0, has_side_effects=True, vmem_limit_bytes=EXCHANGE_VMEM
        ),
        name="exchange",
    )(abundance, spectra, support, panel_blocks)


def per_device(pix_count, eb_count, abundance, spectra, support, panel_blocks):
    rows, cols = abundance.shape
    bands = spectra.shape[1]
    support = support.T
    args = (abundance, spectra, support, panel_blocks)
    if eb_count == 4 and 1 < pix_count and PANEL % (SUB * pix_count) == 0 and rows % (4 * TILE_ROWS) == 0:
        panels, grams, inverse = sums_by_copies(pix_count, *args)
    else:
        panels, grams, inverse = sums_by_collectives(*args)
    params = pltpu.CompilerParams(vmem_limit_bytes=EXCHANGE_VMEM)
    trailing, residual, coefficients = pl.pallas_call(
        update_kernel,
        out_shape=(
            jax.ShapeDtypeStruct((rows, cols), jnp.float32),
            jax.ShapeDtypeStruct((rows, bands), jnp.float32),
            jax.ShapeDtypeStruct((WIDTH, bands), jnp.float32),
        ),
        in_specs=[HBM, HBM, SMEM, HBM, HBM, HBM],
        out_specs=(HBM, HBM, HBM),
        scratch_shapes=[
            pltpu.VMEM((rows, cols), jnp.float32),
            pltpu.VMEM((rows, bands), jnp.float32),
            pltpu.VMEM((rows, WIDTH), jnp.float32),
            pltpu.VMEM(grams.shape, jnp.float32),
            pltpu.VMEM((WIDTH, WIDTH), jnp.float32),
            pltpu.VMEM((WIDTH, bands), jnp.float32),
            pltpu.VMEM((rows, cols), jnp.float32),
            pltpu.VMEM((rows, bands), jnp.float32),
            pltpu.SemaphoreType.DMA((5,)),
            pltpu.SemaphoreType.DMA((rows // TILE_ROWS,)),
            pltpu.SemaphoreType.DMA((rows // TILE_ROWS,)),
            pltpu.SemaphoreType.DMA,
        ],
        compiler_params=params,
        name="update",
    )(abundance, spectra, support, panels, grams, inverse)
    return trailing, residual, coefficients.reshape(NPANELS, PANEL, bands)


def solution(mesh):
    placed = (P("pix", "eb"), P("pix", "eb"), P("pix", "eb"), P())
    return jax.shard_map(
        functools.partial(per_device, mesh.shape["pix"], mesh.shape["eb"]),
        mesh=mesh,
        in_specs=placed,
        out_specs=(P("pix", "eb"), P("pix", "eb"), P(None, None, "eb")),
        check_vma=False,
    )
```

```python
import functools

import jax
import jax.numpy as jnp
from jax import lax
from jax.experimental import pallas as pl
from jax.experimental.pallas import tpu as pltpu
from jax.sharding import PartitionSpec as P

PANEL = 64
TILE_ROWS = 128
NPANELS = 2
WIDTH = PANEL * NPANELS
SUB = 8
VMEM_LIMIT = 48 * 1024 * 1024
EXCHANGE_VMEM = 64 * 1024 * 1024 - 512 * 1024


def product(left, right):
    return jnp.dot(left, right, precision=lax.Precision.HIGHEST, preferred_element_type=jnp.float32)


def product_t(left, right):
    return lax.dot_general(
        left,
        right,
        (((0,), (0,)), ((), ())),
        precision=lax.Precision.HIGHEST,
        preferred_element_type=jnp.float32,
    )


def split(values):
    high = values.astype(jnp.bfloat16)
    return high, (values - high.astype(jnp.float32)).astype(jnp.bfloat16)


def plain(left, right):
    return jnp.dot(left, right, preferred_element_type=jnp.float32)


def product_nt(left, right):
    return lax.dot_general(
        left,
        right,
        (((1,), (1,)), ((), ())),
        precision=lax.Precision.HIGHEST,
        preferred_element_type=jnp.float32,
    )


def support_row(support_ref, tile, cols):
    lane = lax.broadcasted_iota(jnp.int32, (1, cols), 1)
    row = jnp.zeros((1, cols), jnp.float32)
    for block in range(cols // PANEL):
        value = support_ref[block, tile].astype(jnp.float32)
        row = jnp.where((lane >= block * PANEL) & (lane < (block + 1) * PANEL), value, row)
    return row


def inverse_factor(gram):
    shape = (SUB, WIDTH)
    count = PANEL // SUB
    sublane = lax.broadcasted_iota(jnp.int32, shape, 0)
    lane = lax.broadcasted_iota(jnp.int32, shape, 1)
    pad = jnp.concatenate([gram, jnp.zeros_like(gram)], axis=1)
    tiles = [
        pad[i * SUB : (i + 1) * SUB, :] + jnp.where(lane == sublane + (PANEL + i * SUB), 1.0, 0.0)
        for i in range(count)
    ]
    for block in range(count):
        low = block * SUB

        def spread(tile):
            return [jnp.broadcast_to(tile[:, low + j : low + j + 1], shape) for j in range(SUB)]

        rows = tiles[block]
        columns = spread(rows)
        below = {r: spread(tiles[r]) for r in range(block + 1, count)}
        entry = {
            (i, j): jnp.broadcast_to(columns[j][i : i + 1, :], shape)
            for j in range(SUB)
            for i in range(j, SUB)
        }
        g = [jnp.broadcast_to(rows[i : i + 1, :], shape) for i in range(SUB)]
        upper = rows
        for j in range(SUB):
            scale = lax.rsqrt(entry[j, j])
            for i in range(j + 1, SUB):
                entry[i, j] = entry[i, j] * scale
            g[j] = g[j] * scale
            for i in range(j + 1, SUB):
                for k in range(j + 1, i + 1):
                    entry[i, k] = entry[i, k] - entry[i, j] * entry[k, j]
                g[i] = g[i] - entry[i, j] * g[j]
            upper = jnp.where(sublane == j, g[j], upper)
            for r, column in below.items():
                column[j] = column[j] * scale
                for k in range(j + 1, SUB):
                    column[k] = column[k] - column[j] * entry[k, j]
                tiles[r] = tiles[r] - column[j] * g[j]
        tiles[block] = upper
    return jnp.concatenate(tiles, axis=0)[:, PANEL:]


def second_factor(inverse0, grams1, inverse_ref):
    coupling = product_nt(grams1[:, :PANEL], inverse0)
    remainder = grams1[:, PANEL:] - product_nt(coupling, coupling)
    carried = product(coupling, inverse0)
    inverse_ref[:PANEL, :] = jnp.concatenate([inverse0, jnp.zeros_like(inverse0)], axis=1)
    inverse1 = inverse_factor(remainder)
    inverse_ref[PANEL:, :] = jnp.concatenate([-product(inverse1, carried), inverse1], axis=1)


def gram_kernel(x_ref, y_ref, support_ref, c_ref, out_ref):
    rows, cols = x_ref.shape
    total = None
    for tile in range(rows // TILE_ROWS):
        panel = c_ref[tile_span(tile), :]
        masked = masked_tile(x_ref, support_ref, tile)
        joined = jnp.concatenate([masked, y_ref[tile_span(tile), :], panel], axis=1)
        part = product_t(panel, joined)
        total = part if total is None else total + part
    out_ref[...] = total


def factor_kernel(gram_ref, inverse_ref):
    inverse0 = inverse_factor(gram_ref[:PANEL, :PANEL])
    second_factor(inverse0, gram_ref[PANEL:, :], inverse_ref)


def update_kernel(
    x_hbm,
    y_hbm,
    support_hbm,
    c_hbm,
    m_hbm,
    inverse_hbm,
    trail_hbm,
    resid_hbm,
    coef_hbm,
    x_ref,
    y_ref,
    support_ref,
    c_ref,
    m_ref,
    inverse_ref,
    coef,
    trail,
    resid,
    in_sem,
    trail_sem,
    resid_sem,
    coef_sem,
):
    rows, cols = x_ref.shape
    pairs = [(inverse_hbm, inverse_ref), (m_hbm, m_ref), (c_hbm, c_ref), (x_hbm, x_ref), (y_hbm, y_ref)]
    pairs.append((support_hbm, support_ref))
    loads = [pltpu.make_async_copy(src, dst, in_sem.at[index]) for index, (src, dst) in enumerate(pairs)]
    for copy in loads:
        copy.start()
    for copy in loads[:2]:
        copy.wait()
    inverse = inverse_ref[...]
    share = m_ref.shape[1] // NPANELS
    sums = jnp.concatenate(
        [m_ref[p, i * share : (i + 1) * share, :] for i in range(NPANELS) for p in range(m_ref.shape[0])], axis=0
    )
    proj = product(inverse, sums)
    coef[...] = proj[:, cols:]
    stores = [pltpu.make_async_copy(coef, coef_hbm, coef_sem)]
    stores[0].start()
    high, low = split(product_t(inverse, proj))
    weights = jnp.concatenate([high, high, low], axis=0)
    for copy in loads[2:]:
        copy.wait()
    for tile in range(rows // TILE_ROWS):
        span = pl.ds(tile * TILE_ROWS, TILE_ROWS)
        high, low = split(c_ref[span, :])
        change = plain(jnp.concatenate([high, low, high], axis=1), weights)
        trail[span, :] = masked_tile(x_ref, support_ref, tile) - change[:, :cols]
        resid[span, :] = y_ref[span, :] - change[:, cols:]
        stores.append(pltpu.make_async_copy(trail.at[span, :], trail_hbm.at[span, :], trail_sem.at[tile]))
        stores.append(pltpu.make_async_copy(resid.at[span, :], resid_hbm.at[span, :], resid_sem.at[tile]))
        stores[-2].start()
        stores[-1].start()
    for copy in stores:
        copy.wait()


def tile_span(tile):
    start = tile * TILE_ROWS
    return pl.ds(start if isinstance(start, int) else pl.multiple_of(start, TILE_ROWS), TILE_ROWS)


def masked_tile(x_ref, support_ref, tile):
    span = tile_span(tile)
    return x_ref[span, :] * support_row(support_ref, tile, x_ref.shape[1])


def own_panel_pair(x_ref, support_ref, blocks_ref, holder, tile):
    blocks_here = x_ref.shape[1] // PANEL
    left = lax.broadcasted_iota(jnp.int32, (1, WIDTH), 1) < PANEL
    totals = [jnp.zeros((TILE_ROWS, WIDTH), jnp.float32) for _ in range(NPANELS)]
    for place in range(2):
        for pair in range(blocks_here // 2):
            values = x_ref[tile_span(tile + place), pair * WIDTH : (pair + 1) * WIDTH]
            turned = pltpu.roll(values, PANEL, 1)
            for half in range(2):
                local = pair * 2 + half
                keep = support_ref[local, tile + place].astype(jnp.float32)
                source = values if half == place else turned
                for index in range(NPANELS):
                    factor = jnp.where(blocks_ref[index] == holder * blocks_here + local, keep, 0.0)
                    lanes = jnp.where(left, factor, 0.0) if place == 0 else jnp.where(left, 0.0, factor)
                    totals[index] = totals[index] + source * lanes
    return totals


def exchange_kernel(
    pix_count,
    x_hbm,
    y_hbm,
    support_hbm,
    blocks_hbm,
    c_hbm,
    m_ref,
    inverse_ref,
    x_ref,
    y_ref,
    support_ref,
    blocks_ref,
    c_ref,
    own,
    first_in,
    chip_sum,
    second_in,
    full,
    gram0_part,
    gram0,
    gram0_slots,
    gram1_part,
    gram1,
    gram1_slots,
    m0_part,
    m0_slots,
    m1_part,
    m1_slots,
    xy_high,
    xy_low,
    in_sem,
    out_sem,
    send1,
    recv1,
    send2,
    recv2,
    send3,
    recv3,
    gram0_sems,
    gram1_sems,
    m0_sems,
    m1_sems,
    gather_sems,
    near0_sems,
    near1_sems,
):
    rows, cols = x_ref.shape
    half = rows // 2
    chunks = half // (2 * TILE_ROWS)
    pix = lax.axis_index("pix")
    eb = lax.axis_index("eb")
    core = eb % 2
    other_core = 1 - core
    beside = eb + 1 - 2 * core
    across = (eb + 2) % 4
    others = [(pix + d) % pix_count for d in range(1, pix_count)]

    def side_of(ref, side):
        return ref.at[pl.ds(pl.multiple_of(side * half, TILE_ROWS), half), :]

    loads = []
    for index, (src, dst) in enumerate(
        [
            (side_of(x_hbm, other_core), side_of(x_ref, other_core)),
            (side_of(x_hbm, core), side_of(x_ref, core)),
            (y_hbm, y_ref),
            (support_hbm, support_ref),
            (blocks_hbm, blocks_ref),
        ]
    ):
        loads.append(pltpu.make_async_copy(src, dst, in_sem.at[index]))
        loads[-1].start()

    barrier = pltpu.get_barrier_semaphore()
    near = [(pix, (eb + d) % 4) for d in range(1, 4)]
    for target in near + [(other, eb) for other in others]:
        pl.semaphore_signal(barrier, inc=1, device_id=target, device_id_type=pl.DeviceIdType.MESH)

    started = []

    def send(src, dst, send_sem, recv_sem, target):
        copy = pltpu.make_async_remote_copy(
            src_ref=src,
            dst_ref=dst,
            send_sem=send_sem,
            recv_sem=recv_sem,
            device_id=target,
            device_id_type=pl.DeviceIdType.MESH,
        )
        copy.start()
        started.append(copy)
        return copy

    def prepare(side, chunk):
        pair = side * chunks + chunk
        for index, values in enumerate(own_panel_pair(x_ref, support_ref, blocks_ref, eb, pair * 2)):
            own[index, pair] = values

    def pair_span(pair):
        return pl.ds(pl.multiple_of(pair * (2 * TILE_ROWS), 2 * TILE_ROWS), 2 * TILE_ROWS)

    def unpack(index, pair):
        packed = full[index, pair]
        lanes = slice(index * PANEL, (index + 1) * PANEL)
        c_ref[tile_span(pair * 2), lanes] = packed[:, :PANEL]
        c_ref[tile_span(pair * 2 + 1), lanes] = packed[:, PANEL:]

    def gram_of(index):
        return product_t(c_ref[:, index * PANEL : (index + 1) * PANEL], c_ref[...])

    def add_products(index, pair, part, first):
        panel = c_ref[pair_span(pair), index * PANEL : (index + 1) * PANEL]
        high, low = split(panel.T)
        both = plain(jnp.concatenate([high, low], axis=0), xy_high[pair_span(pair), :])
        value = both[:PANEL] + both[PANEL:] + plain(high, xy_low[pair_span(pair), :])
        part[...] = value if first else part[...] + value

    share = PANEL // pix_count
    mine = pl.ds(pl.multiple_of(pix * share, share), share)

    def scatter(part, landing, sems):
        copies = []
        for index, other in enumerate(others):
            rows_there = pl.ds(pl.multiple_of(other * share, share), share)
            copies.append(
                send(part.at[rows_there, :], landing.at[index], sems.at[0, index], sems.at[1, index], (other, eb))
            )
        return copies

    def add_up(part, landing, copies):
        total = part[mine, :]
        for index in range(pix_count - 1):
            copies[index].wait_recv()
            total = total + landing[index]
        return total

    def gather(block, sems, place):
        return [
            send(block, block, sems.at[place, index], sems.at[place + 1, index], (other, eb))
            for index, other in enumerate(others)
        ]

    quarter = PANEL // 4
    here = pl.ds(pl.multiple_of(eb * quarter, quarter), quarter)

    def spread_gram(part, landing, sems):
        return [
            send(part.at[here, :], landing.at[index], sems.at[0, index], sems.at[1, index], (other, eb))
            for index, other in enumerate(others)
        ]

    def share_gram(part, landing, gram, copies, sems):
        total = part[here, :]
        for index in range(pix_count - 1):
            copies[index].wait_recv()
            total = total + landing[index]
        gram[here, :] = total
        return [
            send(gram.at[here, :], gram.at[here, :], sems.at[0, index], sems.at[1, index], target)
            for index, target in enumerate(near)
        ]

    def arrive(index, part):
        copies3 = []
        for chunk in range(chunks):
            copies2[index][chunk].wait_recv()
            pair = core * chunks + chunk
            full[index, pair] = chip_sum[index, chunk] + second_in[index, chunk]
            copies3.append(
                send(
                    full.at[index, pair],
                    full.at[index, pair],
                    send3.at[index, chunk],
                    recv3.at[index, chunk],
                    (pix, beside),
                )
            )
            unpack(index, pair)
            add_products(index, pair, part, chunk == 0)
        for chunk in range(chunks):
            copies3[chunk].wait_recv()
            pair = other_core * chunks + chunk
            unpack(index, pair)
            add_products(index, pair, part, False)

    c_ref[...] = jnp.zeros_like(c_ref)
    loads[3].wait()
    loads[4].wait()
    loads[0].wait()
    for chunk in range(chunks):
        prepare(other_core, chunk)
    pl.semaphore_wait(barrier, pix_count + 2)
    copies1 = [
        [
            send(
                own.at[index, other_core * chunks + chunk],
                first_in.at[index, chunk],
                send1.at[index, chunk],
                recv1.at[index, chunk],
                (pix, beside),
            )
            for chunk in range(chunks)
        ]
        for index in range(NPANELS)
    ]
    loads[1].wait()
    for chunk in range(chunks):
        prepare(core, chunk)
    copies2 = []
    for index in range(NPANELS):
        copies2.append([])
        for chunk in range(chunks):
            copies1[index][chunk].wait_recv()
            chip_sum[index, chunk] = own[index, core * chunks + chunk] + first_in[index, chunk]
            copies2[index].append(
                send(
                    chip_sum.at[index, chunk],
                    second_in.at[index, chunk],
                    send2.at[index, chunk],
                    recv2.at[index, chunk],
                    (pix, across),
                )
            )
    loads[2].wait()
    for tile in range(rows // TILE_ROWS):
        for values, lanes in [
            (masked_tile(x_ref, support_ref, tile), slice(0, cols)),
            (y_ref[tile_span(tile), :], slice(cols, None)),
        ]:
            high, low = split(values)
            xy_high[tile_span(tile), lanes] = high
            xy_low[tile_span(tile), lanes] = low

    low_rows = pl.ds(0, share)
    high_rows = pl.ds(share, share)

    arrive(0, m0_part)
    m0_copies = scatter(m0_part, m0_slots, m0_sems)
    gram0_part[...] = gram_of(0)
    gram0_copies = spread_gram(gram0_part, gram0_slots, gram0_sems)

    arrive(1, m1_part)
    m1_copies = scatter(m1_part, m1_slots, m1_sems)
    gram0_near = share_gram(gram0_part, gram0_slots, gram0, gram0_copies, near0_sems)
    gram1_part[...] = gram_of(1)
    gram1_copies = spread_gram(gram1_part, gram1_slots, gram1_sems)
    keep_c = pltpu.make_async_copy(c_ref, c_hbm, out_sem)
    keep_c.start()
    m_ref[pix, low_rows, :] = add_up(m0_part, m0_slots, m0_copies)
    m0_gather = gather(m_ref.at[pix, low_rows, :], gather_sems, 0)

    for copy in gram0_near:
        copy.wait_recv()
    inverse0 = inverse_factor(gram0[:, :PANEL])
    gram1_near = share_gram(gram1_part, gram1_slots, gram1, gram1_copies, near1_sems)
    m_ref[pix, high_rows, :] = add_up(m1_part, m1_slots, m1_copies)
    m1_gather = gather(m_ref.at[pix, high_rows, :], gather_sems, 2)
    for copy in gram1_near:
        copy.wait_recv()
    second_factor(inverse0, gram1[...], inverse_ref)
    for copy in started[: -len(m1_gather)]:
        copy.wait_send()
    keep_c.wait()
    for copy in m0_gather + m1_gather:
        copy.wait_recv()
    for copy in m1_gather:
        copy.wait_send()


VMEM = pl.BlockSpec(memory_space=pltpu.VMEM)
SMEM = pl.BlockSpec(memory_space=pltpu.SMEM)
HBM = pl.BlockSpec(memory_space=pltpu.HBM)


def own_panels(abundance, support, panel_blocks, holder):
    blocks_here = abundance.shape[1] // PANEL
    parts = []
    for index in range(NPANELS):
        block = panel_blocks[index]
        local = block % blocks_here
        panel = lax.dynamic_slice_in_dim(abundance, local * PANEL, PANEL, 1)
        keep = lax.dynamic_slice_in_dim(support, local, 1, 1).astype(jnp.float32)
        keep = jnp.where(block // blocks_here == holder, keep, 0.0)
        parts.append((panel.reshape(-1, TILE_ROWS, PANEL) * keep[:, :, None]).reshape(-1, PANEL))
    return jnp.concatenate(parts, axis=1)


def sums_by_collectives(abundance, spectra, support, panel_blocks):
    cols = abundance.shape[1]
    bands = spectra.shape[1]
    own = own_panels(abundance, support.T, panel_blocks, lax.axis_index("eb"))
    panels = lax.psum(own, "eb")
    grams = pl.pallas_call(
        gram_kernel,
        out_shape=jax.ShapeDtypeStruct((WIDTH, cols + bands + WIDTH), jnp.float32),
        in_specs=[VMEM, VMEM, SMEM, VMEM],
        out_specs=VMEM,
        compiler_params=pltpu.CompilerParams(vmem_limit_bytes=VMEM_LIMIT),
        name="gram",
    )(abundance, spectra, support, panels)
    grams = lax.psum(grams, "pix")
    inverse = pl.pallas_call(
        factor_kernel,
        out_shape=jax.ShapeDtypeStruct((WIDTH, WIDTH), jnp.float32),
        in_specs=[VMEM],
        out_specs=VMEM,
        compiler_params=pltpu.CompilerParams(vmem_limit_bytes=VMEM_LIMIT),
        name="factor",
    )(grams[:, cols + bands :])
    return panels, grams[:, : cols + bands].reshape(1, WIDTH, cols + bands), inverse


def sums_by_copies(pix_count, abundance, spectra, support, panel_blocks):
    rows, cols = abundance.shape
    width = cols + spectra.shape[1]
    chunks = rows // (4 * TILE_ROWS)
    share = PANEL // pix_count
    away = pix_count - 1
    dma = pltpu.SemaphoreType.DMA

    def buffer(*shape):
        return pltpu.VMEM(shape, jnp.float32)

    return pl.pallas_call(
        functools.partial(exchange_kernel, pix_count),
        out_shape=(
            jax.ShapeDtypeStruct((rows, WIDTH), jnp.float32),
            jax.ShapeDtypeStruct((pix_count, NPANELS * share, width), jnp.float32),
            jax.ShapeDtypeStruct((WIDTH, WIDTH), jnp.float32),
        ),
        in_specs=[HBM, HBM, HBM, HBM],
        out_specs=(HBM, VMEM, VMEM),
        scratch_shapes=[
            buffer(*abundance.shape),
            buffer(*spectra.shape),
            pltpu.SMEM(support.shape, jnp.int32),
            pltpu.SMEM(panel_blocks.shape, jnp.int32),
            buffer(rows, WIDTH),
            buffer(NPANELS, 2 * chunks, TILE_ROWS, WIDTH),
            buffer(NPANELS, chunks, TILE_ROWS, WIDTH),
            buffer(NPANELS, chunks, TILE_ROWS, WIDTH),
            buffer(NPANELS, chunks, TILE_ROWS, WIDTH),
            buffer(NPANELS, 2 * chunks, TILE_ROWS, WIDTH),
            buffer(PANEL, WIDTH),
            buffer(PANEL, WIDTH),
            buffer(away, PANEL // 4, WIDTH),
            buffer(PANEL, WIDTH),
            buffer(PANEL, WIDTH),
            buffer(away, PANEL // 4, WIDTH),
            buffer(PANEL, width),
            buffer(away, share, width),
            buffer(PANEL, width),
            buffer(away, share, width),
            pltpu.VMEM((rows, width), jnp.bfloat16),
            pltpu.VMEM((rows, width), jnp.bfloat16),
            dma((5,)),
            dma,
        ]
        + [dma((NPANELS, chunks))] * 6
        + [dma((2, away))] * 4
        + [dma((4, away)), dma((2, 3)), dma((2, 3))],
        compiler_params=pltpu.CompilerParams(
            collective_id=0, has_side_effects=True, vmem_limit_bytes=EXCHANGE_VMEM
        ),
        name="exchange",
    )(abundance, spectra, support, panel_blocks)


def per_device(pix_count, eb_count, abundance, spectra, support, panel_blocks):
    rows, cols = abundance.shape
    bands = spectra.shape[1]
    support = support.T
    args = (abundance, spectra, support, panel_blocks)
    if eb_count == 4 and 1 < pix_count and PANEL % (SUB * pix_count) == 0 and rows % (4 * TILE_ROWS) == 0:
        panels, grams, inverse = sums_by_copies(pix_count, *args)
    else:
        panels, grams, inverse = sums_by_collectives(*args)
    params = pltpu.CompilerParams(vmem_limit_bytes=EXCHANGE_VMEM)
    trailing, residual, coefficients = pl.pallas_call(
        update_kernel,
        out_shape=(
            jax.ShapeDtypeStruct((rows, cols), jnp.float32),
            jax.ShapeDtypeStruct((rows, bands), jnp.float32),
            jax.ShapeDtypeStruct((WIDTH, bands), jnp.float32),
        ),
        in_specs=[HBM] * 6,
        out_specs=(HBM, HBM, HBM),
        scratch_shapes=[
            pltpu.VMEM((rows, cols), jnp.float32),
            pltpu.VMEM((rows, bands), jnp.float32),
            pltpu.SMEM(support.shape, jnp.int32),
            pltpu.VMEM((rows, WIDTH), jnp.float32),
            pltpu.VMEM(grams.shape, jnp.float32),
            pltpu.VMEM((WIDTH, WIDTH), jnp.float32),
            pltpu.VMEM((WIDTH, bands), jnp.float32),
            pltpu.VMEM((rows, cols), jnp.float32),
            pltpu.VMEM((rows, bands), jnp.float32),
            pltpu.SemaphoreType.DMA((6,)),
            pltpu.SemaphoreType.DMA((rows // TILE_ROWS,)),
            pltpu.SemaphoreType.DMA((rows // TILE_ROWS,)),
            pltpu.SemaphoreType.DMA,
        ],
        compiler_params=params,
        name="update",
    )(abundance, spectra, support, panels, grams, inverse)
    return trailing, residual, coefficients.reshape(NPANELS, PANEL, bands)


def solution(mesh):
    placed = (P("pix", "eb"), P("pix", "eb"), P("pix", "eb"), P())
    return jax.shard_map(
        functools.partial(per_device, mesh.shape["pix"], mesh.shape["eb"]),
        mesh=mesh,
        in_specs=placed,
        out_specs=(P("pix", "eb"), P("pix", "eb"), P(None, None, "eb")),
        check_vma=False,
    )
```
